32 devices in a mesh: parts: 2 (over y), gx: 8 (over z, x), gy: 2 (over core).
Axes of the slice: x: 2, y: 2, z: 4, core: 2. Of those that a mesh axis runs over, the one named last changes fastest.
Arguments:
- conc: float32 [12, 256, 2, 256], P(None, ('parts', 'gx'), None, 'gy'), parts along dimension 1, may hold values from 0.1 to 2
- sens: float32 [8, 12, 256, 2, 256], P(None, None, ('parts', 'gx'), None, 'gy'), parts along dimension 2, may hold values from -6 to 6
- vel_x: float32 [256, 2, 256], P(('parts', 'gx'), None, 'gy'), parts along dimension 0, may hold values from 0.3 to 1
- vel_y: float32 [256, 2, 256], P(('parts', 'gx'), None, 'gy'), parts along dimension 0, may hold values from 0.3 to 1
- up_x: int32 [256, 2, 256], P(('parts', 'gx'), None, 'gy'), parts along dimension 0, may hold values 0 or 1
- up_y: int32 [256, 2, 256], P(('parts', 'gx'), None, 'gy'), parts along dimension 0, may hold values 0 or 1
- sorb_zone: int32 [256, 2, 256], P(('parts', 'gx'), None, 'gy'), parts along dimension 0, may hold values from 0 to 2
- rate_zone: int32 [256, 2, 256], P(('parts', 'gx'), None, 'gy'), parts along dimension 0, may hold values from 0 to 7
- param_values: float32 [8], replicated, may hold values from 0.1 to 0.5
- mol_diff: float32 [12], replicated, may hold values from 0.02 to 0.2
- sorb_cap: float32 [12], replicated, may hold values from 0.2 to 2
- rate_table: float32 [8, 3], replicated, may hold values from 0.5 to 2
- exch_matrix: float32 [12, 12], replicated, may hold values from -1.75 to 1.75
- stoich: float32 [12, 3], replicated, may hold values from -2 to 2
Outputs:
- conc_out: float32 [12, 256, 2, 256], P(None, ('parts', 'gx'), None, 'gy'), parts along dimension 1
- sens_out: float32 [8, 12, 256, 2, 256], P(None, None, ('parts', 'gx'), None, 'gy'), parts along dimension 2
The draws below stay inside these ranges and needn't reach their ends.
There are 2 independent parts, one for each index of `parts`. The reference program is written for one: setup_inputs(seed, part) draws one part's arguments, and reference() takes and returns one part's arrays. A program takes and returns all parts, laid end to end along the dimension named above; an argument that names none is the same for every part. Nothing has to cross between parts.
All inputs are finite; a program needn't handle non-finite values. No bound on the sum of `up_x` or of `up_y` on one device may be relied on, other than what follows from the above.
Results may differ from the reference program's by a relative error of at most 0.000078.
Values sent between devices are 32-bit elements; how exact they have to be, the bound alone decides.
A program may use at most 64 MiB of HBM per device.

```python
import math
import jax
import jax.numpy as jnp
from jax import lax

LAYERS = 2
NC = 12
NP = 8
NR = 3
SZONES = 3
RZONES = 8
NX = 128
NY = 256


def touch_ends(values, key, least, top_value):
    place = [jax.random.randint(jax.random.fold_in(key, axis), (), 0, length) for axis, length in enumerate(values.shape)]
    longest = values.shape.index(max(values.shape))
    next_to = place[:longest] + [(place[longest] + 1) % values.shape[longest]] + place[longest + 1:]
    return values.at[tuple(place)].set(least).at[tuple(next_to)].set(top_value)


def block_scale(own_key, extent, split, low, largest):
    loudness = 1.0
    for position, blocks in split:
        heights = jax.random.uniform(jax.random.fold_in(jax.random.fold_in(own_key, 6), position), (blocks,), jnp.float32, low / len(split), largest / len(split))
        loudness = loudness * jnp.repeat(jnp.exp(heights), extent[position] // blocks).reshape((-1,) + (1,) * (len(extent) - 1 - position))
    return loudness


def noise(rng, extent, width, limit, shards=(), held_as=jnp.bfloat16):
    result = width * jax.random.normal(rng, extent, jnp.float32)
    if shards:
        result = result * block_scale(rng, extent, shards, -0.22, 0.18)
    return jnp.clip(result, -limit, limit).astype(held_as)


def setup_inputs(seed: int = 0, part: int = 0) -> dict:
    keys = jax.random.split(jax.random.key(seed), 15)
    part_keys = jax.random.split(jax.random.fold_in(keys[14], part), 15)
    conc = jnp.clip(0.1 + 1.9 * jax.random.uniform(part_keys[0], (NC, NX, LAYERS, NY), jnp.float32) ** block_scale(part_keys[0], (NC, NX, LAYERS, NY), ((1, 8), (3, 2)), -0.2, 0.2), 0.1, 2.0)
    sens = noise(part_keys[1], (NP, NC, NX, LAYERS, NY), 1.0, 6.0, ((2, 8), (4, 2)), jnp.float32)
    vel_x = jnp.clip(jnp.exp(math.log(1.0) - 1.2039728 * jax.random.uniform(part_keys[2], (NX, LAYERS, NY), jnp.float32) ** block_scale(part_keys[2], (NX, LAYERS, NY), ((0, 8), (2, 2)), -0.2, 0.2)), 0.3, 1.0)
    vel_y = jnp.clip(jnp.exp(math.log(1.0) - 1.2039728 * jax.random.uniform(part_keys[3], (NX, LAYERS, NY), jnp.float32) ** block_scale(part_keys[3], (NX, LAYERS, NY), ((0, 8), (2, 2)), -0.2, 0.2)), 0.3, 1.0)
    up_x = touch_ends((jax.random.randint(part_keys[4], (NX, LAYERS, NY), 0, 2) < 1).astype(jnp.int32), jax.random.fold_in(part_keys[4], 1), 0, 1)
    up_y = touch_ends((jax.random.randint(part_keys[5], (NX, LAYERS, NY), 0, 2) < 1).astype(jnp.int32), jax.random.fold_in(part_keys[5], 1), 0, 1)
    sorb_zone = touch_ends(jax.random.randint(part_keys[6], (NX, LAYERS, NY), 0, SZONES), jax.random.fold_in(part_keys[6], 1), 0, SZONES - 1).astype(jnp.int32)
    rate_zone = touch_ends(jax.random.randint(part_keys[7], (NX, LAYERS, NY), 0, RZONES), jax.random.fold_in(part_keys[7], 1), 0, RZONES - 1).astype(jnp.int32)
    param_values = jnp.clip(jnp.exp(jax.random.uniform(keys[8], (NP,), jnp.float32, math.log(0.1), math.log(0.5))), 0.1, 0.5)
    mol_diff = jnp.clip(jnp.exp(jax.random.uniform(keys[9], (NC,), jnp.float32, math.log(0.02), math.log(0.2))), 0.02, 0.2)
    sorb_cap = jnp.clip(jnp.exp(jax.random.uniform(keys[10], (NC,), jnp.float32, math.log(0.2), math.log(2.0))), 0.2, 2.0)
    rate_table = jnp.clip(jnp.exp(jax.random.uniform(keys[11], (RZONES, NR), jnp.float32, math.log(0.5), math.log(2.0))), 0.5, 2.0)
    exch_matrix = noise(keys[12], (NC, NC), NC ** -0.5, 1.75, (), jnp.float32)
    stoich = noise(keys[13], (NC, NR), 0.5, 2.0, (), jnp.float32)
    return {"conc": conc, "sens": sens, "vel_x": vel_x, "vel_y": vel_y, "up_x": up_x, "up_y": up_y, "sorb_zone": sorb_zone, "rate_zone": rate_zone, "param_values": param_values, "mol_diff": mol_diff, "sorb_cap": sorb_cap, "rate_table": rate_table, "exch_matrix": exch_matrix, "stoich": stoich}


DISP_STEP = 0.25
COURANT = 0.2
REACT_STEP = 0.2


def cell_fields(vel_x, vel_y, up_x, up_y, sorb_zone, rate_zone, rate_table):
    sorb_ids = jnp.arange(SZONES, dtype=jnp.int32)
    rate_ids = jnp.arange(RZONES, dtype=jnp.int32)
    sorb_onehot = (sorb_zone[None] == sorb_ids[:, None, None, None]).astype(jnp.float32)
    rate_onehot = (rate_zone[None] == rate_ids[:, None, None, None]).astype(jnp.float32)
    zone_rates = jnp.einsum("zr,zxly->rxly", rate_table.astype(jnp.float32), rate_onehot, precision=lax.Precision.HIGHEST)
    return jnp.concatenate([vel_x[None], vel_y[None], up_x.astype(jnp.float32)[None], up_y.astype(jnp.float32)[None], sorb_onehot, zone_rates], 0)


def pad_state(full):
    return jnp.pad(full, ((0, 0), (0, 0), (1, 1), (0, 0), (1, 1)))


def pad_fields(fields):
    return jnp.pad(fields, ((0, 0), (1, 1), (0, 0), (1, 1)))


def disperse(full, padded, fields, param_values, mol_diff):
    lap_x = padded[:, :, 2:, :, 1:-1] + padded[:, :, :-2, :, 1:-1] - 2.0 * full
    lap_y = padded[:, :, 1:-1, :, 2:] + padded[:, :, 1:-1, :, :-2] - 2.0 * full
    lap_z = full[:, :, :, ::-1, :] - full
    molec = mol_diff[:, None, None, None]
    coef_x = param_values[0] * fields[0] + molec
    coef_y = param_values[1] * fields[1] + molec
    moved = full + DISP_STEP * (coef_x * lap_x + coef_y * lap_y + molec * lap_z)
    moved = moved.at[1].add(DISP_STEP * fields[0] * lap_x[0])
    moved = moved.at[2].add(DISP_STEP * fields[1] * lap_y[0])
    return moved


def advect(full, padded, fields, frame, param_values, sorb_cap):
    low_x = padded[:, :, :-2, :, 1:-1]
    high_x = padded[:, :, 2:, :, 1:-1]
    low_y = padded[:, :, 1:-1, :, :-2]
    high_y = padded[:, :, 1:-1, :, 2:]
    next_speed_x = frame[0, 2:, :, 1:-1]
    next_mask_x = frame[2, 2:, :, 1:-1]
    next_speed_y = frame[1, 1:-1, :, 2:]
    next_mask_y = frame[3, 1:-1, :, 2:]
    flux_low_x = fields[0] * (fields[2] * low_x - (1.0 - fields[2]) * full)
    flux_high_x = next_speed_x * (next_mask_x * full - (1.0 - next_mask_x) * high_x)
    flux_low_y = fields[1] * (fields[3] * low_y - (1.0 - fields[3]) * full)
    flux_high_y = next_speed_y * (next_mask_y * full - (1.0 - next_mask_y) * high_y)
    diverge = flux_high_x - flux_low_x + flux_high_y - flux_low_y
    sorb_onehot = fields[4:4 + SZONES]
    sorb_param = jnp.sum(sorb_onehot * param_values[5:5 + SZONES][:, None, None, None], 0)
    capacity = sorb_cap[:, None, None, None]
    retard = 1.0 + sorb_param[None] * capacity
    moved = full - COURANT * diverge / retard
    for zone in range(SZONES):
        moved = moved.at[6 + zone].add(COURANT * capacity * sorb_onehot[zone] * diverge[0] / (retard * retard))
    return moved


def react(full, fields, param_values, exch_matrix, stoich):
    zone_rates = fields[4 + SZONES:4 + SZONES + NR]
    primal = full[0]
    linear = jnp.einsum("cd,kdxly->kcxly", exch_matrix, full, precision=lax.Precision.HIGHEST)
    rate_list = []
    for react_idx in range(NR):
        donor = 2 * react_idx
        accept = 2 * react_idx + 1
        factor = param_values[2 + react_idx] * zone_rates[react_idx]
        prim_rate = factor * primal[donor] * primal[accept]
        tang_rate = factor * (primal[accept] * full[1:, donor] + primal[donor] * full[1:, accept])
        rate_list.append(jnp.concatenate([prim_rate[None], tang_rate], 0))
    rates = jnp.stack(rate_list, 1)
    chem = jnp.einsum("cr,krxly->kcxly", stoich, rates, precision=lax.Precision.HIGHEST)
    reacted = full + REACT_STEP * (linear + chem)
    for react_idx in range(NR):
        donor = 2 * react_idx
        accept = 2 * react_idx + 1
        source = zone_rates[react_idx] * primal[donor] * primal[accept]
        reacted = reacted.at[3 + react_idx].add(REACT_STEP * stoich[:, react_idx][:, None, None, None] * source[None])
    return reacted


def reference(conc, sens, vel_x, vel_y, up_x, up_y, sorb_zone, rate_zone, param_values, mol_diff, sorb_cap, rate_table, exch_matrix, stoich):
    full = jnp.concatenate([conc[None], sens], 0)
    fields = cell_fields(vel_x, vel_y, up_x, up_y, sorb_zone, rate_zone, rate_table)
    frame = pad_fields(fields[:4])
    full = disperse(full, pad_state(full), fields, param_values, mol_diff)
    full = advect(full, pad_state(full), fields, frame, param_values, sorb_cap)
    full = react(full, fields, param_values, exch_matrix, stoich)
    full = disperse(full, pad_state(full), fields, param_values, mol_diff)
    return full[0], full[1:]
```

```python
import functools
import jax
import jax.numpy as jnp
from jax import lax
from jax.experimental import pallas as pl
from jax.experimental.pallas import tpu as pltpu
from jax.sharding import PartitionSpec as P

NC = 12
NP = 8
NK = NP + 1
NR = 3
SZONES = 3
RZONES = 8
GROUPS = 3
PER = NC // GROUPS
HALO = 2 * PER * NK

DISP_STEP = 0.25
COURANT = 0.2
REACT_STEP = 0.2
PAD = 8


def kernel(
    rows,
    lanes,
    conc_ref,
    sens_ref,
    vx_ref,
    vy_ref,
    ux_ref,
    uy_ref,
    sz_ref,
    rz_ref,
    p_ref,
    mol_ref,
    cap_ref,
    table_ref,
    exch_ref,
    stoich_ref,
    conc_out,
    sens_out,
    sta,
    stb,
    xsend,
    xrecv,
    ysend,
    yrecv,
    vsend,
    vrecv,
    fields,
    load_sem,
    xs_sem,
    xr_sem,
    ys_sem,
    yr_sem,
    vs_sem,
    vr_sem,
):
    gx = lax.axis_index("gx")
    gy = lax.axis_index("gy")
    ngx = lax.axis_size("gx")
    has_lo = gx > 0
    has_hi = gx < ngx - 1
    body = pl.ds(PAD, rows)

    loads = [pltpu.make_async_copy(conc_ref, sta.at[0, :, body, :], load_sem.at[0])]
    loads.append(pltpu.make_async_copy(sens_ref, sta.at[pl.ds(1, NP), :, body, :], load_sem.at[1]))
    for copy in loads:
        copy.start()

    barrier = pltpu.get_barrier_semaphore()
    pl.semaphore_signal(barrier, inc=1, device_id={"gy": 1 - gy})

    @pl.when(has_lo)
    def _():
        pl.semaphore_signal(barrier, inc=1, device_id={"gx": gx - 1})

    @pl.when(has_hi)
    def _():
        pl.semaphore_signal(barrier, inc=1, device_id={"gx": gx + 1})

    lane = lax.broadcasted_iota(jnp.int32, (rows, lanes), 1)
    row = lax.broadcasted_iota(jnp.int32, (rows, lanes), 0)
    even = (row % 2) == 0
    inner_lane = jnp.where(gy == 0, lanes - 1, 0)
    first = lane == 0
    last = lane == lanes - 1
    inner = lane == inner_lane

    vx = vx_ref[...]
    vy = vy_ref[...]
    ux = ux_ref[...].astype(jnp.float32)
    uy = uy_ref[...].astype(jnp.float32)
    vsend[0:2, :] = vx[0:2]
    vsend[2:4, :] = ux[0:2]

    @pl.when(jnp.logical_not(has_lo))
    def _():
        xrecv[:, 0] = jnp.zeros_like(xrecv[:, 0])

    @pl.when(jnp.logical_not(has_hi))
    def _():
        xrecv[:, 1] = jnp.zeros_like(xrecv[:, 1])
        vrecv[...] = jnp.zeros_like(vrecv)


    def lo_copy(stage):
        return pltpu.make_async_remote_copy(
            src_ref=xsend.at[stage, 0],
            dst_ref=xrecv.at[stage, 1],
            send_sem=xs_sem.at[stage, 0],
            recv_sem=xr_sem.at[stage, 1],
            device_id={"gx": gx - 1},
        )

    def hi_copy(stage):
        return pltpu.make_async_remote_copy(
            src_ref=xsend.at[stage, 1],
            dst_ref=xrecv.at[stage, 0],
            send_sem=xs_sem.at[stage, 1],
            recv_sem=xr_sem.at[stage, 0],
            device_id={"gx": gx + 1},
        )

    def y_copy(stage):
        return pltpu.make_async_remote_copy(
            src_ref=ysend.at[stage],
            dst_ref=yrecv.at[stage],
            send_sem=ys_sem.at[stage],
            recv_sem=yr_sem.at[stage],
            device_id={"gy": 1 - gy},
        )

    v_copy = pltpu.make_async_remote_copy(
        src_ref=vsend,
        dst_ref=vrecv,
        send_sem=vs_sem,
        recv_sem=vr_sem,
        device_id={"gx": gx - 1},
    )

    def send_x(src, stage):
        def step(g, carry):
            for j in range(PER):
                c = g * PER + j
                for k in range(NK):
                    off = 2 * (j * NK + k)
                    xsend[stage, 0, g, off : off + 2, :] = src[k, c, PAD : PAD + 2, :]
                    xsend[stage, 1, g, off : off + 2, :] = src[k, c, PAD + rows - 2 : PAD + rows, :]
            return carry

        lax.fori_loop(0, GROUPS, step, 0)

        @pl.when(has_lo)
        def _():
            lo_copy(stage).start()

        @pl.when(has_hi)
        def _():
            hi_copy(stage).start()

    def send_y(src, stage, start):
        def step(g, acc):
            for j in range(PER):
                c = g * PER + j
                for k in range(NK):
                    slot = c * NK + k
                    shift = lax.rem(slot - inner_lane + lanes, lanes)
                    moved = pltpu.roll(src[k, c, body, :], shift, 1)
                    acc = jnp.where(lane == slot, moved, acc)
            return acc

        ysend[stage] = lax.fori_loop(0, GROUPS, step, start)
        y_copy(stage).start()

    def receive(dst, stage):
        @pl.when(has_lo)
        def _():
            hi_copy(stage).wait_recv()

        @pl.when(has_hi)
        def _():
            lo_copy(stage).wait_recv()

        y_copy(stage).wait_recv()

        def step(g, carry):
            for j in range(PER):
                c = g * PER + j
                for k in range(NK):
                    off = 2 * (j * NK + k)
                    dst[k, c, PAD - 2 : PAD, :] = xrecv[stage, 0, g, off : off + 2, :]
                    dst[k, c, PAD + rows : PAD + rows + 2, :] = xrecv[stage, 1, g, off : off + 2, :]
            return carry

        lax.fori_loop(0, GROUPS, step, 0)

    def y_halo(stage, slot):
        return pltpu.roll(yrecv[stage], lax.rem(inner_lane - slot + lanes, lanes), 1)

    def disperse(src, stage, put):
        def step(c, carry):
            m = DISP_STEP * mol_ref[c]
            cx = fields[0] + m
            cy = fields[1] + m
            c0 = 1.0 - 2.0 * cx - 2.0 * cy - m
            cyl = jnp.where(first, 0.0, cy)
            cyh = jnp.where(last, 0.0, cy)
            cyi = jnp.where(inner, cy, 0.0)
            for k in range(NK):
                v = src[k, c, body, :]
                sx = src[k, c, PAD - 2 : PAD - 2 + rows, :] + src[k, c, PAD + 2 : PAD + 2 + rows, :]
                other = jnp.where(
                    even,
                    src[k, c, PAD + 1 : PAD + 1 + rows, :],
                    src[k, c, PAD - 1 : PAD - 1 + rows, :],
                )
                yl = pltpu.roll(v, 1, 1)
                yh = pltpu.roll(v, lanes - 1, 1)
                yi = y_halo(stage, c * NK + k)
                out = c0 * v + cx * sx + m * other + cyl * yl + cyh * yh + cyi * yi
                if k == 0:
                    lap_x = sx - 2.0 * v
                    lap_y = (
                        jnp.where(first, 0.0, yl)
                        + jnp.where(last, 0.0, yh)
                        + jnp.where(inner, yi, 0.0)
                        - 2.0 * v
                    )
                if k == 1:
                    out = out + DISP_STEP * vx_ref[...] * lap_x
                if k == 2:
                    out = out + DISP_STEP * vy_ref[...] * lap_y
                put(k, c, out)
            return carry

        lax.fori_loop(0, NC, step, 0)

    def put_stb(k, c, out):
        stb[k, c, body, :] = out

    def put_out(k, c, out):
        if k == 0:
            conc_out[c] = out
        else:
            sens_out[k - 1, c] = out

    fields[0] = DISP_STEP * p_ref[0] * vx
    fields[1] = DISP_STEP * p_ref[1] * vy

    y_start = jnp.where(
        lane == NK * NC,
        pltpu.roll(vy, lax.rem(NK * NC - inner_lane + lanes, lanes), 1),
        pltpu.roll(uy, lax.rem(NK * NC + 1 - inner_lane + lanes, lanes), 1),
    )

    for copy in loads:
        copy.wait()

    count = 1 + has_lo.astype(jnp.int32) + has_hi.astype(jnp.int32)
    pl.semaphore_wait(barrier, count)

    @pl.when(has_lo)
    def _():
        v_copy.start()

    send_x(sta, 0)
    send_y(sta, 0, y_start)
    receive(sta, 0)
    disperse(sta, 0, put_stb)

    send_x(stb, 1)
    send_y(stb, 1, jnp.zeros((rows, lanes), jnp.float32))

    @pl.when(has_hi)
    def _():
        v_copy.wait_recv()

    vx_next = jnp.concatenate([vx[2:], vrecv[0:2, :]], 0)
    ux_next = jnp.concatenate([ux[2:], vrecv[2:4, :]], 0)
    open_hi = gy == 0
    edge = jnp.where(open_hi, lanes - 1, 0)
    vy_in = pltpu.roll(yrecv[0], lax.rem(edge - NK * NC + lanes, lanes), 1)
    uy_in = pltpu.roll(yrecv[0], lax.rem(edge - NK * NC - 1 + lanes, lanes), 1)
    keep = jnp.where(open_hi, 1.0, 0.0)
    vy_next = jnp.where(last, vy_in * keep, pltpu.roll(vy, lanes - 1, 1))
    uy_next = jnp.where(last, uy_in * keep, pltpu.roll(uy, lanes - 1, 1))
    axl = vx * ux
    axh = vx_next * (1.0 - ux_next)
    ayl = vy * uy
    ayh = vy_next * (1.0 - uy_next)
    fields[2] = vx_next * ux_next + vx * (1.0 - ux) + vy_next * uy_next + vy * (1.0 - uy)
    fields[3] = axl
    fields[4] = axh
    fields[5] = jnp.where(first, 0.0, ayl)
    fields[6] = jnp.where(last, 0.0, ayh)
    fields[7] = jnp.where(inner, keep * ayh + (1.0 - keep) * ayl, 0.0)
    sorb_zone = sz_ref[...]
    sorb = jnp.zeros((rows, lanes), jnp.float32)
    for z in range(SZONES):
        sorb = jnp.where(sorb_zone == z, p_ref[5 + z], sorb)
    fields[8] = sorb
    rate_zone = rz_ref[...]
    for r in range(NR):
        rate = jnp.zeros((rows, lanes), jnp.float32)
        for z in range(RZONES):
            rate = jnp.where(rate_zone == z, table_ref[r, z], rate)
        fields[9 + r] = rate

    receive(stb, 1)

    def advect(c, carry):
        cap = cap_ref[c]
        retard = 1.0 + fields[8] * cap
        scale = COURANT / retard
        for k in range(NK):
            v = stb[k, c, body, :]
            div = (
                fields[2] * v
                - fields[3] * stb[k, c, PAD - 2 : PAD - 2 + rows, :]
                - fields[4] * stb[k, c, PAD + 2 : PAD + 2 + rows, :]
                - fields[5] * pltpu.roll(v, 1, 1)
                - fields[6] * pltpu.roll(v, lanes - 1, 1)
                - fields[7] * y_halo(1, c * NK + k)
            )
            out = v - scale * div
            if k == 0:
                extra = cap * div * (scale / retard)
            if k >= 6:
                out = out + jnp.where(sz_ref[...] == k - 6, extra, 0.0)
            sta[k, c, body, :] = out
        return carry

    lax.fori_loop(0, NC, advect, 0)

    half = rows // 2
    for h in range(2):
        part = pl.ds(PAD + h * half, half)
        fpart = pl.ds(h * half, half)
        s = [sta[0, c, part, :] for c in range(2 * NR)]
        source = [fields[9 + r, fpart, :] * s[2 * r] * s[2 * r + 1] for r in range(NR)]

        def mix(k, v, q):
            for c in range(NC):
                acc = exch_ref[c, 0] * v[0]
                for d in range(1, NC):
                    acc = acc + exch_ref[c, d] * v[d]
                for r in range(NR):
                    acc = acc + stoich_ref[r, c] * q[r]
                sta[k, c, part, :] = v[c] + REACT_STEP * acc

        def tangent(k, carry):
            v = [sta[k, c, part, :] for c in range(NC)]
            q = []
            for r in range(NR):
                factor = p_ref[2 + r] * fields[9 + r, fpart, :]
                flag = jnp.where(k == 3 + r, 1.0, 0.0)
                q.append(factor * (s[2 * r + 1] * v[2 * r] + s[2 * r] * v[2 * r + 1]) + flag * source[r])
            mix(k, v, q)
            return carry

        lax.fori_loop(1, NK, tangent, 0)
        mix(0, [sta[0, c, part, :] for c in range(NC)], [p_ref[2 + r] * source[r] for r in range(NR)])

    send_x(sta, 2)
    send_y(sta, 2, jnp.zeros((rows, lanes), jnp.float32))
    receive(sta, 2)
    disperse(sta, 2, put_out)

    for stage in range(3):
        y_copy(stage).wait_send()

    @pl.when(has_lo)
    def _():
        for stage in range(3):
            lo_copy(stage).wait_send()
        v_copy.wait_send()

    @pl.when(has_hi)
    def _():
        for stage in range(3):
            hi_copy(stage).wait_send()


def on_device(
    conc,
    sens,
    vel_x,
    vel_y,
    up_x,
    up_y,
    sorb_zone,
    rate_zone,
    param_values,
    mol_diff,
    sorb_cap,
    rate_table,
    exch_matrix,
    stoich,
):
    nx, layers, ny = vel_x.shape
    rows = nx * layers
    flat = lambda a: a.reshape(a.shape[:-3] + (rows, ny))
    vmem = pl.BlockSpec(memory_space=pltpu.VMEM)
    smem = pl.BlockSpec(memory_space=pltpu.SMEM)
    hbm = pl.BlockSpec(memory_space=pl.ANY)
    f32 = jnp.float32
    state = (NK, NC, rows + 2 * PAD, ny)
    conc_out, sens_out = pl.pallas_call(
        functools.partial(kernel, rows, ny),
        out_shape=(
            jax.ShapeDtypeStruct((NC, rows, ny), f32),
            jax.ShapeDtypeStruct((NP, NC, rows, ny), f32),
        ),
        in_specs=[hbm, hbm] + [vmem] * 6 + [smem] * 6,
        out_specs=(vmem, vmem),
        scratch_shapes=[
            pltpu.VMEM(state, f32),
            pltpu.VMEM(state, f32),
            pltpu.VMEM((3, 2, GROUPS, HALO, ny), f32),
            pltpu.VMEM((3, 2, GROUPS, HALO, ny), f32),
            pltpu.VMEM((3, rows, ny), f32),
            pltpu.VMEM((3, rows, ny), f32),
            pltpu.VMEM((8, ny), f32),
            pltpu.VMEM((8, ny), f32),
            pltpu.VMEM((12, rows, ny), f32),
            pltpu.SemaphoreType.DMA((2,)),
            pltpu.SemaphoreType.DMA((3, 2)),
            pltpu.SemaphoreType.DMA((3, 2)),
            pltpu.SemaphoreType.DMA((3,)),
            pltpu.SemaphoreType.DMA((3,)),
            pltpu.SemaphoreType.DMA,
            pltpu.SemaphoreType.DMA,
        ],
        compiler_params=pltpu.CompilerParams(
            collective_id=0, has_side_effects=True, vmem_limit_bytes=62 * 1024 * 1024
        ),
    )(
        flat(conc),
        flat(sens),
        flat(vel_x),
        flat(vel_y),
        flat(up_x),
        flat(up_y),
        flat(sorb_zone),
        flat(rate_zone),
        param_values,
        mol_diff,
        sorb_cap,
        jnp.transpose(rate_table),
        exch_matrix,
        jnp.transpose(stoich),
    )
    return conc_out.reshape(conc.shape), sens_out.reshape(sens.shape)


def solution(mesh):
    cell = P(("parts", "gx"), None, "gy")
    outs = (P(None, ("parts", "gx"), None, "gy"), P(None, None, ("parts", "gx"), None, "gy"))
    return jax.shard_map(
        on_device,
        mesh=mesh,
        in_specs=outs + (cell,) * 6 + (P(),) * 6,
        out_specs=outs,
        check_vma=False,
    )
```

```python
import functools
import jax
import jax.numpy as jnp
from jax import lax
from jax.experimental import pallas as pl
from jax.experimental.pallas import tpu as pltpu
from jax.sharding import PartitionSpec as P

NC = 12
NP = 8
NK = NP + 1
NR = 3
SZONES = 3
RZONES = 8

DISP_STEP = 0.25
COURANT = 0.2
REACT_STEP = 0.2

BASE = 12
EXT = 8
HALO = 6


def kernel(
    rows,
    lanes,
    conc_ref,
    sens_ref,
    vx_ref,
    vy_ref,
    ux_ref,
    uy_ref,
    sz_ref,
    rz_ref,
    p_ref,
    mol_ref,
    cap_ref,
    table_ref,
    exch_ref,
    stoich_ref,
    conc_out,
    sens_out,
    inbuf,
    outbuf,
    sta,
    stb,
    xsend,
    xrecv,
    ysend,
    yrecv,
    fsend,
    frecv,
    cells,
    disp,
    adv,
    scale,
    rates,
    state,
    extra_d,
    extra_a,
    load_sem,
    store_sem,
    xs_sem,
    xr_sem,
    ys_sem,
    yr_sem,
    fs_sem,
    fr_sem,
):
    gx = lax.axis_index("gx")
    gy = lax.axis_index("gy")
    ngx = lax.axis_size("gx")
    has_lo = gx > 0
    has_hi = gx < ngx - 1
    wide = rows + 2 * (BASE - EXT)
    f32 = jnp.float32

    def load(k):
        return pltpu.make_async_copy(sens_ref.at[k - 1], inbuf.at[k], load_sem.at[k])

    load_first = pltpu.make_async_copy(conc_ref, inbuf.at[0], load_sem.at[0])
    load_first.start()
    for k in range(1, NK):
        load(k).start()

    barrier = pltpu.get_barrier_semaphore()
    pl.semaphore_signal(barrier, inc=1, device_id={"gy": 1 - gy})

    @pl.when(has_lo)
    def _():
        pl.semaphore_signal(barrier, inc=1, device_id={"gx": gx - 1})

    @pl.when(has_hi)
    def _():
        pl.semaphore_signal(barrier, inc=1, device_id={"gx": gx + 1})

    own = (
        vx_ref[...],
        vy_ref[...],
        ux_ref[...].astype(f32),
        uy_ref[...].astype(f32),
        sz_ref[...].astype(f32),
        rz_ref[...].astype(f32),
    )
    for f in range(6):
        fsend[0, HALO * f : HALO * (f + 1), :] = own[f][0:HALO]
        fsend[1, HALO * f : HALO * (f + 1), :] = own[f][rows - HALO : rows]
        cells[f, BASE : BASE + rows, :] = own[f]

    @pl.when(jnp.logical_not(has_lo))
    def _():
        xrecv[:, 0] = jnp.zeros_like(xrecv[:, 0])
        frecv[0] = jnp.zeros_like(frecv[0])

    @pl.when(jnp.logical_not(has_hi))
    def _():
        xrecv[:, 1] = jnp.zeros_like(xrecv[:, 1])
        frecv[1] = jnp.zeros_like(frecv[1])

    def x_copy(k, side):
        return pltpu.make_async_remote_copy(
            src_ref=xsend.at[k, side],
            dst_ref=xrecv.at[k, 1 - side],
            send_sem=xs_sem.at[k, side],
            recv_sem=xr_sem.at[k, 1 - side],
            device_id={"gx": gx - 1 if side == 0 else gx + 1},
        )

    def f_copy(side):
        return pltpu.make_async_remote_copy(
            src_ref=fsend.at[side],
            dst_ref=frecv.at[1 - side],
            send_sem=fs_sem.at[side],
            recv_sem=fr_sem.at[1 - side],
            device_id={"gx": gx - 1 if side == 0 else gx + 1},
        )

    def y_copy(stage, k):
        return pltpu.make_async_remote_copy(
            src_ref=ysend.at[stage, k],
            dst_ref=yrecv.at[stage, k],
            send_sem=ys_sem.at[stage, k],
            recv_sem=yr_sem.at[stage, k],
            device_id={"gy": 1 - gy},
        )

    count = 1 + has_lo.astype(jnp.int32) + has_hi.astype(jnp.int32)
    pl.semaphore_wait(barrier, count)

    @pl.when(has_lo)
    def _():
        f_copy(0).start()

    @pl.when(has_hi)
    def _():
        f_copy(1).start()

    def send(k):
        for c in range(NC):
            xsend[k, 0, HALO * c : HALO * (c + 1), :] = inbuf[k, c, 0:HALO, :]
            xsend[k, 1, HALO * c : HALO * (c + 1), :] = inbuf[k, c, rows - HALO : rows, :]

        @pl.when(has_lo)
        def _():
            x_copy(k, 0).start()

        @pl.when(has_hi)
        def _():
            x_copy(k, 1).start()

    load_first.wait()
    send(0)

    def send_step(k, carry):
        load(k).wait()
        send(k)
        return carry

    lax.fori_loop(1, NK, send_step, 0)

    @pl.when(has_lo)
    def _():
        f_copy(1).wait_recv()

    @pl.when(has_hi)
    def _():
        f_copy(0).wait_recv()

    for f in range(6):
        cells[f, BASE - HALO : BASE, :] = frecv[0, HALO * f : HALO * (f + 1), :]
        cells[f, BASE + rows : BASE + rows + HALO, :] = frecv[1, HALO * f : HALO * (f + 1), :]

    lane = lax.broadcasted_iota(jnp.int32, (wide, lanes), 1)
    row = lax.broadcasted_iota(jnp.int32, (wide, lanes), 0)
    even = (row % 2) == 0
    inner_lane = jnp.where(gy == 0, lanes - 1, 0)
    first = lane == 0
    last = lane == lanes - 1
    inner = lane == inner_lane
    margin = BASE - EXT
    lo_ok = jnp.where(has_lo, 1.0, 0.0)
    hi_ok = jnp.where(has_hi, 1.0, 0.0)
    valid = jnp.where(row < margin, lo_ok, jnp.where(row >= margin + rows, hi_ok, 1.0))
    ext = pl.ds(EXT, wide)

    fx = DISP_STEP * p_ref[0] * cells[0, ext, :]
    fy = DISP_STEP * p_ref[1] * cells[1, ext, :]
    sorb = jnp.zeros((wide, lanes), f32)
    for z in range(SZONES):
        sorb = jnp.where(cells[4, ext, :] == float(z), p_ref[5 + z], sorb)

    def coefficients(c, carry):
        m = DISP_STEP * mol_ref[c]
        cx = (fx + m) * valid
        cy = (fy + m) * valid
        cm = m * valid
        disp[0, c] = valid - 2.0 * cx - 2.0 * cy - cm
        disp[1, c] = cx
        disp[2, c] = cm
        disp[3, c] = jnp.where(first, 0.0, cy)
        disp[4, c] = jnp.where(last, 0.0, cy)
        disp[5, c] = jnp.where(inner, cy, 0.0)
        scale[c] = valid * COURANT / (1.0 + sorb * cap_ref[c])
        for stage in range(2):
            extra_d[stage, 0, c] = jnp.zeros((wide, lanes), f32)
        return carry

    lax.fori_loop(0, NC, coefficients, 0)
    for r in range(NR):
        rate = jnp.zeros((wide, lanes), f32)
        for z in range(RZONES):
            rate = jnp.where(cells[5, ext, :] == float(z), table_ref[r, z], rate)
        rates[r] = rate

    def pack(acc, v, slot):
        moved = pltpu.roll(v, lax.rem(slot - inner_lane + lanes, lanes), 1)
        return jnp.where(lane == slot, moved, acc)

    def unpack(stage, k, slot, span):
        return pltpu.roll(yrecv[stage, k, span, :], lax.rem(inner_lane - slot + lanes, lanes), 1)

    def enter(k):
        @pl.when(has_lo)
        def _():
            x_copy(k, 1).wait_recv()

        @pl.when(has_hi)
        def _():
            x_copy(k, 0).wait_recv()

        acc = pack(jnp.zeros((wide, lanes), f32), cells[1, ext, :], NC)
        acc = pack(acc, cells[3, ext, :], NC + 1)
        for c in range(NC):
            sta[k, c, BASE : BASE + rows, :] = inbuf[k, c]
            sta[k, c, BASE - HALO : BASE, :] = xrecv[k, 0, HALO * c : HALO * (c + 1), :]
            sta[k, c, BASE + rows : BASE + rows + HALO, :] = xrecv[k, 1, HALO * c : HALO * (c + 1), :]
            acc = pack(acc, sta[k, c, ext, :], c)
        ysend[0, k] = acc
        y_copy(0, k).start()

    def disperse(src, stage, which, k, start, count, put):
        y_copy(stage, k).wait_recv()
        inside = pl.ds(start - EXT, count)
        cut = slice(start - EXT, start - EXT + count)

        def near(c, kk):
            v = src[kk, c, start : start + count, :]
            sx = src[kk, c, start - 2 : start - 2 + count, :] + src[kk, c, start + 2 : start + 2 + count, :]
            return v, sx

        @pl.when(k == 0)
        def _():
            for c in range(NC):
                v, sx = near(c, 0)
                lap_y = (
                    jnp.where(first[cut], 0.0, pltpu.roll(v, 1, 1))
                    + jnp.where(last[cut], 0.0, pltpu.roll(v, lanes - 1, 1))
                    + jnp.where(inner[cut], unpack(stage, 0, c, inside), 0.0)
                    - 2.0 * v
                )
                part = DISP_STEP * valid[cut]
                extra_d[which, 1, c, inside, :] = part * cells[0, start : start + count, :] * (sx - 2.0 * v)
                extra_d[which, 2, c, inside, :] = part * cells[1, start : start + count, :] * lap_y

        index = jnp.where(k == 1, 1, jnp.where(k == 2, 2, 0))
        acc = jnp.zeros((count, lanes), f32)
        for c in range(NC):
            v, sx = near(c, k)
            other = jnp.where(
                even[cut],
                src[k, c, start + 1 : start + 1 + count, :],
                src[k, c, start - 1 : start - 1 + count, :],
            )
            out = (
                disp[0, c, inside, :] * v
                + disp[1, c, inside, :] * sx
                + disp[2, c, inside, :] * other
                + disp[3, c, inside, :] * pltpu.roll(v, 1, 1)
                + disp[4, c, inside, :] * pltpu.roll(v, lanes - 1, 1)
                + disp[5, c, inside, :] * unpack(stage, k, c, inside)
                + extra_d[which, index, c, inside, :]
            )
            put(k, c, out)
            if which == 0:
                acc = pack(acc, out, c)
        if which == 0:
            ysend[1, k] = acc
            y_copy(1, k).start()

    def put_stb(k, c, out):
        stb[k, c, ext, :] = out

    def put_out(k, c, out):
        outbuf[k, c] = out

    def advection_fields():
        keep = jnp.where(gy == 0, 1.0, 0.0)
        vx, vy, ux, uy = [cells[f, ext, :] for f in range(4)]
        ahead = pl.ds(EXT + 2, wide)
        vx_next = cells[0, ahead, :]
        ux_next = cells[2, ahead, :]
        shift = lambda slot: pltpu.roll(yrecv[0, 0], lanes - 1 - slot, 1)
        vy_next = jnp.where(last, shift(NC) * keep, pltpu.roll(vy, lanes - 1, 1))
        uy_next = jnp.where(last, shift(NC + 1) * keep, pltpu.roll(uy, lanes - 1, 1))
        ayl = vy * uy
        ayh = vy_next * (1.0 - uy_next)
        adv[0] = vx_next * ux_next + vx * (1.0 - ux) + vy_next * uy_next + vy * (1.0 - uy)
        adv[1] = vx * ux
        adv[2] = vx_next * (1.0 - ux_next)
        adv[3] = jnp.where(first, 0.0, ayl)
        adv[4] = jnp.where(last, 0.0, ayh)
        adv[5] = jnp.where(inner, keep * ayh + (1.0 - keep) * ayl, 0.0)

    def divergence(k, c):
        v = stb[k, c, ext, :]
        div = (
            adv[0] * v
            - adv[1] * stb[k, c, EXT - 2 : EXT - 2 + wide, :]
            - adv[2] * stb[k, c, EXT + 2 : EXT + 2 + wide, :]
            - adv[3] * pltpu.roll(v, 1, 1)
            - adv[4] * pltpu.roll(v, lanes - 1, 1)
            - adv[5] * unpack(1, k, c, slice(None))
        )
        return v, div

    def advect(k):
        y_copy(1, k).wait_recv()

        @pl.when(k == 0)
        def _():
            advection_fields()
            for c in range(NC):
                v, div = divergence(0, c)
                step = scale[c]
                extra_a[c] = div * (cap_ref[c] / COURANT) * step * step
                if c < 2 * NR:
                    state[c] = v - step * div

        here = cells[4, ext, :] == (k - 6).astype(f32)
        for c in range(NC):
            v, div = divergence(k, c)
            sta[k, c, ext, :] = v - scale[c] * div + jnp.where(here, extra_a[c], 0.0)

        half = jnp.where(k == 0, 0.5, 1.0)
        for start, count in ((0, 24), (24, wide - 24)):
            part = pl.ds(EXT + start, count)
            inside = pl.ds(start, count)
            v = [sta[k, c, part, :] for c in range(NC)]
            q = []
            for r in range(NR):
                donor = state[2 * r, inside, :]
                accept = state[2 * r + 1, inside, :]
                rate = rates[r, inside, :]
                flag = jnp.where(k == 3 + r, 1.0, 0.0)
                both = accept * v[2 * r] + donor * v[2 * r + 1]
                q.append(rate * ((p_ref[2 + r] * half) * both + flag * (donor * accept)))
            for c in range(NC):
                acc = exch_ref[c, 0] * v[0]
                for d in range(1, NC):
                    acc = acc + exch_ref[c, d] * v[d]
                for r in range(NR):
                    acc = acc + stoich_ref[r, c] * q[r]
                sta[k, c, part, :] = v[c] + REACT_STEP * acc

        acc = jnp.zeros((wide, lanes), f32)
        for c in range(NC):
            acc = pack(acc, sta[k, c, ext, :], c)
        ysend[2, k] = acc
        y_copy(2, k).start()

    def store_first():
        return pltpu.make_async_copy(outbuf.at[0], conc_out, store_sem.at[0])

    def store(k):
        return pltpu.make_async_copy(outbuf.at[k], sens_out.at[k - 1], store_sem.at[k])

    def leave(k):
        disperse(sta, 2, 1, k, BASE, rows, put_out)

        @pl.when(k == 0)
        def _():
            store_first().start()

        @pl.when(k > 0)
        def _():
            store(k).start()

    def turn(t, carry):
        @pl.when(t < NK)
        def _():
            enter(t)

        @pl.when(jnp.logical_and(t >= 1, t < NK + 1))
        def _():
            disperse(sta, 0, 0, t - 1, EXT, wide, put_stb)

        @pl.when(jnp.logical_and(t >= 2, t < NK + 2))
        def _():
            advect(t - 2)

        @pl.when(t >= 3)
        def _():
            leave(t - 3)

        return carry

    lax.fori_loop(0, NK + 3, turn, 0)

    def finish(k, carry):
        for stage in range(3):
            y_copy(stage, k).wait_send()

        @pl.when(has_lo)
        def _():
            x_copy(k, 0).wait_send()

        @pl.when(has_hi)
        def _():
            x_copy(k, 1).wait_send()

        return carry

    lax.fori_loop(0, NK, finish, 0)

    @pl.when(has_lo)
    def _():
        f_copy(0).wait_send()

    @pl.when(has_hi)
    def _():
        f_copy(1).wait_send()

    store_first().wait()
    for k in range(1, NK):
        store(k).wait()


def on_device(
    conc,
    sens,
    vel_x,
    vel_y,
    up_x,
    up_y,
    sorb_zone,
    rate_zone,
    param_values,
    mol_diff,
    sorb_cap,
    rate_table,
    exch_matrix,
    stoich,
):
    nx, layers, ny = vel_x.shape
    rows = nx * layers
    wide = rows + 2 * (BASE - EXT)
    tall = rows + 2 * BASE
    flat = lambda a: a.reshape(a.shape[:-3] + (rows, ny))
    vmem = pl.BlockSpec(memory_space=pltpu.VMEM)
    smem = pl.BlockSpec(memory_space=pltpu.SMEM)
    hbm = pl.BlockSpec(memory_space=pl.ANY)
    f32 = jnp.float32
    dma = pltpu.SemaphoreType.DMA
    conc_out, sens_out = pl.pallas_call(
        functools.partial(kernel, rows, ny),
        out_shape=(
            jax.ShapeDtypeStruct((NC, rows, ny), f32),
            jax.ShapeDtypeStruct((NP, NC, rows, ny), f32),
        ),
        in_specs=[hbm, hbm] + [vmem] * 6 + [smem] * 6,
        out_specs=(hbm, hbm),
        scratch_shapes=[
            pltpu.VMEM((NK, NC, rows, ny), f32),
            pltpu.VMEM((NK, NC, rows, ny), f32),
            pltpu.VMEM((NK, NC, tall, ny), f32),
            pltpu.VMEM((NK, NC, tall, ny), f32),
            pltpu.VMEM((NK, 2, HALO * NC, ny), f32),
            pltpu.VMEM((NK, 2, HALO * NC, ny), f32),
            pltpu.VMEM((3, NK, wide, ny), f32),
            pltpu.VMEM((3, NK, wide, ny), f32),
            pltpu.VMEM((2, 40, ny), f32),
            pltpu.VMEM((2, 40, ny), f32),
            pltpu.VMEM((6, tall, ny), f32),
            pltpu.VMEM((6, NC, wide, ny), f32),
            pltpu.VMEM((6, wide, ny), f32),
            pltpu.VMEM((NC, wide, ny), f32),
            pltpu.VMEM((NR, wide, ny), f32),
            pltpu.VMEM((2 * NR, wide, ny), f32),
            pltpu.VMEM((2, 3, NC, wide, ny), f32),
            pltpu.VMEM((NC, wide, ny), f32),
            dma((NK,)),
            dma((NK,)),
            dma((NK, 2)),
            dma((NK, 2)),
            dma((3, NK)),
            dma((3, NK)),
            dma((2,)),
            dma((2,)),
        ],
        compiler_params=pltpu.CompilerParams(
            collective_id=0, has_side_effects=True, vmem_limit_bytes=62 * 1024 * 1024
        ),
    )(
        flat(conc),
        flat(sens),
        flat(vel_x),
        flat(vel_y),
        flat(up_x),
        flat(up_y),
        flat(sorb_zone),
        flat(rate_zone),
        param_values,
        mol_diff,
        sorb_cap,
        jnp.transpose(rate_table),
        exch_matrix,
        jnp.transpose(stoich),
    )
    return conc_out.reshape(conc.shape), sens_out.reshape(sens.shape)


def solution(mesh):
    cell = P(("parts", "gx"), None, "gy")
    outs = (P(None, ("parts", "gx"), None, "gy"), P(None, None, ("parts", "gx"), None, "gy"))
    return jax.shard_map(
        on_device,
        mesh=mesh,
        in_specs=outs + (cell,) * 6 + (P(),) * 6,
        out_specs=outs,
        check_vma=False,
    )
```

```python
import functools
import jax
import jax.numpy as jnp
from jax import lax
from jax.experimental import pallas as pl
from jax.experimental.pallas import tpu as pltpu
from jax.sharding import PartitionSpec as P

NC = 12
NP = 8
NK = NP + 1
NR = 3
SZONES = 3
RZONES = 8

DISP_STEP = 0.25
COURANT = 0.2
REACT_STEP = 0.2

BASE = 12
EXT = 8
HALO = 6
AHEAD = 3


def kernel(
    rows,
    lanes,
    conc_ref,
    sens_ref,
    vx_ref,
    vy_ref,
    ux_ref,
    uy_ref,
    sz_ref,
    rz_ref,
    p_ref,
    mol_ref,
    cap_ref,
    table_ref,
    exch_ref,
    stoich_ref,
    conc_out,
    sens_out,
    inbuf,
    outbuf,
    sta,
    stb,
    stc,
    xsend,
    xrecv,
    yrecv,
    fsend,
    frecv,
    yfields,
    cells,
    disp,
    adv,
    scale,
    rates,
    state,
    extra_d,
    extra_a,
    load_sem,
    store_sem,
    xs_sem,
    xr_sem,
    ys_sem,
    yr_sem,
    fs_sem,
    fr_sem,
    yfs_sem,
    yfr_sem,
):
    gx = lax.axis_index("gx")
    gy = lax.axis_index("gy")
    ngx = lax.axis_size("gx")
    has_lo = gx > 0
    has_hi = gx < ngx - 1
    wide = rows + 2 * (BASE - EXT)
    f32 = jnp.float32

    def load(k):
        return pltpu.make_async_copy(sens_ref.at[k - 1], inbuf.at[k], load_sem.at[k])

    load_first = pltpu.make_async_copy(conc_ref, inbuf.at[0], load_sem.at[0])
    load_first.start()
    for k in range(1, NK):
        load(k).start()

    barrier = pltpu.get_barrier_semaphore()
    pl.semaphore_signal(barrier, inc=1, device_id={"gy": 1 - gy})

    @pl.when(has_lo)
    def _():
        pl.semaphore_signal(barrier, inc=1, device_id={"gx": gx - 1})

    @pl.when(has_hi)
    def _():
        pl.semaphore_signal(barrier, inc=1, device_id={"gx": gx + 1})

    own = (
        vx_ref[...],
        vy_ref[...],
        ux_ref[...].astype(f32),
        uy_ref[...].astype(f32),
        sz_ref[...].astype(f32),
        rz_ref[...].astype(f32),
    )
    for f in range(6):
        fsend[0, HALO * f : HALO * (f + 1), :] = own[f][0:HALO]
        fsend[1, HALO * f : HALO * (f + 1), :] = own[f][rows - HALO : rows]
        cells[f, BASE : BASE + rows, :] = own[f]

    @pl.when(jnp.logical_not(has_lo))
    def _():
        xrecv[:, 0] = jnp.zeros_like(xrecv[:, 0])
        frecv[0] = jnp.zeros_like(frecv[0])

    @pl.when(jnp.logical_not(has_hi))
    def _():
        xrecv[:, 1] = jnp.zeros_like(xrecv[:, 1])
        frecv[1] = jnp.zeros_like(frecv[1])

    def x_copy(k, side):
        return pltpu.make_async_remote_copy(
            src_ref=xsend.at[k, side],
            dst_ref=xrecv.at[k, 1 - side],
            send_sem=xs_sem.at[k, side],
            recv_sem=xr_sem.at[k, 1 - side],
            device_id={"gx": gx - 1 if side == 0 else gx + 1},
        )

    def f_copy(side):
        return pltpu.make_async_remote_copy(
            src_ref=fsend.at[side],
            dst_ref=frecv.at[1 - side],
            send_sem=fs_sem.at[side],
            recv_sem=fr_sem.at[1 - side],
            device_id={"gx": gx - 1 if side == 0 else gx + 1},
        )

    ext = pl.ds(EXT, wide)

    def y_copy(stage, k):
        return pltpu.make_async_remote_copy(
            src_ref=(sta, stb, stc)[stage].at[k, :, ext, :],
            dst_ref=yrecv.at[stage, k],
            send_sem=ys_sem.at[stage, k],
            recv_sem=yr_sem.at[stage, k],
            device_id={"gy": 1 - gy},
        )

    yf_copy = pltpu.make_async_remote_copy(
        src_ref=cells.at[:, ext, :],
        dst_ref=yfields,
        send_sem=yfs_sem,
        recv_sem=yfr_sem,
        device_id={"gy": 1 - gy},
    )

    count = 1 + has_lo.astype(jnp.int32) + has_hi.astype(jnp.int32)
    pl.semaphore_wait(barrier, count)

    @pl.when(has_lo)
    def _():
        f_copy(0).start()

    @pl.when(has_hi)
    def _():
        f_copy(1).start()

    def send(k):
        for c in range(NC):
            xsend[k, 0, HALO * c : HALO * (c + 1), :] = inbuf[k, c, 0:HALO, :]
            xsend[k, 1, HALO * c : HALO * (c + 1), :] = inbuf[k, c, rows - HALO : rows, :]

        @pl.when(has_lo)
        def _():
            x_copy(k, 0).start()

        @pl.when(has_hi)
        def _():
            x_copy(k, 1).start()

    load_first.wait()
    send(0)

    def send_step(k, carry):
        load(k).wait()
        send(k)
        return carry

    lax.fori_loop(1, AHEAD, send_step, 0)

    @pl.when(has_lo)
    def _():
        f_copy(1).wait_recv()

    @pl.when(has_hi)
    def _():
        f_copy(0).wait_recv()

    for f in range(6):
        cells[f, BASE - HALO : BASE, :] = frecv[0, HALO * f : HALO * (f + 1), :]
        cells[f, BASE + rows : BASE + rows + HALO, :] = frecv[1, HALO * f : HALO * (f + 1), :]

    yf_copy.start()

    lane = lax.broadcasted_iota(jnp.int32, (wide, lanes), 1)
    row = lax.broadcasted_iota(jnp.int32, (wide, lanes), 0)
    even = (row % 2) == 0
    first = lane == 0
    last = lane == lanes - 1
    no_lo = jnp.logical_and(first, gy == 0)
    no_hi = jnp.logical_and(last, gy == 1)
    from_lo = jnp.logical_and(last, gy == 1)
    from_hi = jnp.logical_and(first, gy == 0)
    margin = BASE - EXT
    lo_ok = jnp.where(has_lo, 1.0, 0.0)
    hi_ok = jnp.where(has_hi, 1.0, 0.0)
    valid = jnp.where(row < margin, lo_ok, jnp.where(row >= margin + rows, hi_ok, 1.0))
    fx = DISP_STEP * p_ref[0] * cells[0, ext, :]
    fy = DISP_STEP * p_ref[1] * cells[1, ext, :]
    sorb = jnp.zeros((wide, lanes), f32)
    for z in range(SZONES):
        sorb = jnp.where(cells[4, ext, :] == float(z), p_ref[5 + z], sorb)

    def coefficients(c, carry):
        m = DISP_STEP * mol_ref[c]
        cx = (fx + m) * valid
        cy = (fy + m) * valid
        cm = m * valid
        disp[0, c] = valid - 2.0 * cx - 2.0 * cy - cm
        disp[1, c] = cx
        disp[2, c] = cm
        disp[3, c] = jnp.where(no_lo, 0.0, cy)
        disp[4, c] = jnp.where(no_hi, 0.0, cy)
        scale[c] = valid * COURANT / (1.0 + sorb * cap_ref[c])
        for stage in range(2):
            extra_d[stage, 0, c] = jnp.zeros((wide, lanes), f32)
        return carry

    lax.fori_loop(0, NC, coefficients, 0)
    for r in range(NR):
        rate = jnp.zeros((wide, lanes), f32)
        for z in range(RZONES):
            rate = jnp.where(cells[5, ext, :] == float(z), table_ref[r, z], rate)
        rates[r] = rate

    def y_near(v, stage, k, c, span, cut):
        other = yrecv[stage, k, c, span, :]
        low = pltpu.roll(jnp.where(from_lo[cut], other, v), 1, 1)
        high = pltpu.roll(jnp.where(from_hi[cut], other, v), lanes - 1, 1)
        return low, high

    def enter(k):
        @pl.when(has_lo)
        def _():
            x_copy(k, 1).wait_recv()

        @pl.when(has_hi)
        def _():
            x_copy(k, 0).wait_recv()

        for c in range(NC):
            sta[k, c, BASE : BASE + rows, :] = inbuf[k, c]
            sta[k, c, BASE - HALO : BASE, :] = xrecv[k, 0, HALO * c : HALO * (c + 1), :]
            sta[k, c, BASE + rows : BASE + rows + HALO, :] = xrecv[k, 1, HALO * c : HALO * (c + 1), :]
        y_copy(0, k).start()

        @pl.when(k + AHEAD < NK)
        def _():
            load(k + AHEAD).wait()
            send(k + AHEAD)

    def disperse(src, stage, which, k, start, count, put):
        y_copy(stage, k).wait_recv()
        inside = pl.ds(start - EXT, count)
        cut = slice(start - EXT, start - EXT + count)

        def near(c, kk):
            v = src[kk, c, start : start + count, :]
            sx = src[kk, c, start - 2 : start - 2 + count, :] + src[kk, c, start + 2 : start + 2 + count, :]
            return v, sx

        @pl.when(k == 0)
        def _():
            for c in range(NC):
                v, sx = near(c, 0)
                yl, yh = y_near(v, stage, 0, c, inside, cut)
                lap_y = jnp.where(no_lo[cut], 0.0, yl) + jnp.where(no_hi[cut], 0.0, yh) - 2.0 * v
                part = DISP_STEP * valid[cut]
                extra_d[which, 1, c, inside, :] = part * cells[0, start : start + count, :] * (sx - 2.0 * v)
                extra_d[which, 2, c, inside, :] = part * cells[1, start : start + count, :] * lap_y

        index = jnp.where(k == 1, 1, jnp.where(k == 2, 2, 0))
        for c in range(NC):
            v, sx = near(c, k)
            yl, yh = y_near(v, stage, k, c, inside, cut)
            other = jnp.where(
                even[cut],
                src[k, c, start + 1 : start + 1 + count, :],
                src[k, c, start - 1 : start - 1 + count, :],
            )
            out = (
                disp[0, c, inside, :] * v
                + disp[1, c, inside, :] * sx
                + disp[2, c, inside, :] * other
                + disp[3, c, inside, :] * yl
                + disp[4, c, inside, :] * yh
                + extra_d[which, index, c, inside, :]
            )
            put(k, c, out)
        if which == 0:
            y_copy(1, k).start()

    def put_stb(k, c, out):
        stb[k, c, ext, :] = out

    def put_out(k, c, out):
        outbuf[k, c] = out

    def advection_fields():
        keep = jnp.where(gy == 0, 1.0, 0.0)
        vx, vy, ux, uy = [cells[f, ext, :] for f in range(4)]
        ahead = pl.ds(EXT + 2, wide)
        vx_next = cells[0, ahead, :]
        ux_next = cells[2, ahead, :]
        yf_copy.wait_recv()
        vy_next = jnp.where(last, keep, 1.0) * pltpu.roll(jnp.where(from_hi, yfields[1], vy), lanes - 1, 1)
        uy_next = jnp.where(last, keep, 1.0) * pltpu.roll(jnp.where(from_hi, yfields[3], uy), lanes - 1, 1)
        ayl = vy * uy
        ayh = vy_next * (1.0 - uy_next)
        adv[0] = vx_next * ux_next + vx * (1.0 - ux) + vy_next * uy_next + vy * (1.0 - uy)
        adv[1] = vx * ux
        adv[2] = vx_next * (1.0 - ux_next)
        adv[3] = jnp.where(no_lo, 0.0, ayl)
        adv[4] = jnp.where(no_hi, 0.0, ayh)

    def divergence(k, c):
        v = stb[k, c, ext, :]
        yl, yh = y_near(v, 1, k, c, slice(None), slice(None))
        div = (
            adv[0] * v
            - adv[1] * stb[k, c, EXT - 2 : EXT - 2 + wide, :]
            - adv[2] * stb[k, c, EXT + 2 : EXT + 2 + wide, :]
            - adv[3] * yl
            - adv[4] * yh
        )
        return v, div

    def advect(k):
        y_copy(1, k).wait_recv()

        @pl.when(k == 0)
        def _():
            advection_fields()
            for c in range(NC):
                v, div = divergence(0, c)
                step = scale[c]
                extra_a[c] = div * (cap_ref[c] / COURANT) * step * step
                if c < 2 * NR:
                    state[c] = v - step * div

        here = cells[4, ext, :] == (k - 6).astype(f32)
        for c in range(NC):
            v, div = divergence(k, c)
            stc[k, c, ext, :] = v - scale[c] * div + jnp.where(here, extra_a[c], 0.0)

        half = jnp.where(k == 0, 0.5, 1.0)
        for start, count in ((0, 24), (24, wide - 24)):
            part = pl.ds(EXT + start, count)
            inside = pl.ds(start, count)
            v = [stc[k, c, part, :] for c in range(NC)]
            q = []
            for r in range(NR):
                donor = state[2 * r, inside, :]
                accept = state[2 * r + 1, inside, :]
                rate = rates[r, inside, :]
                flag = jnp.where(k == 3 + r, 1.0, 0.0)
                both = accept * v[2 * r] + donor * v[2 * r + 1]
                q.append(rate * ((p_ref[2 + r] * half) * both + flag * (donor * accept)))
            for c in range(NC):
                acc = exch_ref[c, 0] * v[0]
                for d in range(1, NC):
                    acc = acc + exch_ref[c, d] * v[d]
                for r in range(NR):
                    acc = acc + stoich_ref[r, c] * q[r]
                stc[k, c, part, :] = v[c] + REACT_STEP * acc

        y_copy(2, k).start()

    def store_first():
        return pltpu.make_async_copy(outbuf.at[0], conc_out, store_sem.at[0])

    def store(k):
        return pltpu.make_async_copy(outbuf.at[k], sens_out.at[k - 1], store_sem.at[k])

    def leave(k):
        disperse(stc, 2, 1, k, BASE, rows, put_out)

        @pl.when(k == 0)
        def _():
            store_first().start()

        @pl.when(k > 0)
        def _():
            store(k).start()

    def turn(t, carry):
        @pl.when(t < NK)
        def _():
            enter(t)

        @pl.when(jnp.logical_and(t >= 1, t < NK + 1))
        def _():
            disperse(sta, 0, 0, t - 1, EXT, wide, put_stb)

        @pl.when(jnp.logical_and(t >= 2, t < NK + 2))
        def _():
            advect(t - 2)

        @pl.when(t >= 3)
        def _():
            leave(t - 3)

        return carry

    lax.fori_loop(0, NK + 3, turn, 0)

    def finish(k, carry):
        for stage in range(3):
            y_copy(stage, k).wait_send()

        @pl.when(has_lo)
        def _():
            x_copy(k, 0).wait_send()

        @pl.when(has_hi)
        def _():
            x_copy(k, 1).wait_send()

        return carry

    lax.fori_loop(0, NK, finish, 0)
    yf_copy.wait_send()

    @pl.when(has_lo)
    def _():
        f_copy(0).wait_send()

    @pl.when(has_hi)
    def _():
        f_copy(1).wait_send()

    store_first().wait()
    for k in range(1, NK):
        store(k).wait()


def on_device(
    conc,
    sens,
    vel_x,
    vel_y,
    up_x,
    up_y,
    sorb_zone,
    rate_zone,
    param_values,
    mol_diff,
    sorb_cap,
    rate_table,
    exch_matrix,
    stoich,
):
    nx, layers, ny = vel_x.shape
    rows = nx * layers
    wide = rows + 2 * (BASE - EXT)
    tall = rows + 2 * BASE
    flat = lambda a: a.reshape(a.shape[:-3] + (rows, ny))
    vmem = pl.BlockSpec(memory_space=pltpu.VMEM)
    smem = pl.BlockSpec(memory_space=pltpu.SMEM)
    hbm = pl.BlockSpec(memory_space=pl.ANY)
    f32 = jnp.float32
    dma = pltpu.SemaphoreType.DMA
    conc_out, sens_out = pl.pallas_call(
        functools.partial(kernel, rows, ny),
        out_shape=(
            jax.ShapeDtypeStruct((NC, rows, ny), f32),
            jax.ShapeDtypeStruct((NP, NC, rows, ny), f32),
        ),
        in_specs=[hbm, hbm] + [vmem] * 6 + [smem] * 6,
        out_specs=(hbm, hbm),
        scratch_shapes=[
            pltpu.VMEM((NK, NC, rows, ny), f32),
            pltpu.VMEM((NK, NC, rows, ny), f32),
            pltpu.VMEM((NK, NC, tall, ny), f32),
            pltpu.VMEM((NK, NC, tall, ny), f32),
            pltpu.VMEM((NK, NC, tall, ny), f32),
            pltpu.VMEM((NK, 2, HALO * NC, ny), f32),
            pltpu.VMEM((NK, 2, HALO * NC, ny), f32),
            pltpu.VMEM((3, NK, NC, wide, ny), f32),
            pltpu.VMEM((2, 40, ny), f32),
            pltpu.VMEM((2, 40, ny), f32),
            pltpu.VMEM((6, wide, ny), f32),
            pltpu.VMEM((6, tall, ny), f32),
            pltpu.VMEM((5, NC, wide, ny), f32),
            pltpu.VMEM((5, wide, ny), f32),
            pltpu.VMEM((NC, wide, ny), f32),
            pltpu.VMEM((NR, wide, ny), f32),
            pltpu.VMEM((2 * NR, wide, ny), f32),
            pltpu.VMEM((2, 3, NC, wide, ny), f32),
            pltpu.VMEM((NC, wide, ny), f32),
            dma((NK,)),
            dma((NK,)),
            dma((NK, 2)),
            dma((NK, 2)),
            dma((3, NK)),
            dma((3, NK)),
            dma((2,)),
            dma((2,)),
            dma,
            dma,
        ],
        compiler_params=pltpu.CompilerParams(
            collective_id=0, has_side_effects=True, vmem_limit_bytes=62 * 1024 * 1024
        ),
    )(
        flat(conc),
        flat(sens),
        flat(vel_x),
        flat(vel_y),
        flat(up_x),
        flat(up_y),
        flat(sorb_zone),
        flat(rate_zone),
        param_values,
        mol_diff,
        sorb_cap,
        jnp.transpose(rate_table),
        exch_matrix,
        jnp.transpose(stoich),
    )
    return conc_out.reshape(conc.shape), sens_out.reshape(sens.shape)


def solution(mesh):
    cell = P(("parts", "gx"), None, "gy")
    outs = (P(None, ("parts", "gx"), None, "gy"), P(None, None, ("parts", "gx"), None, "gy"))
    return jax.shard_map(
        on_device,
        mesh=mesh,
        in_specs=outs + (cell,) * 6 + (P(),) * 6,
        out_specs=outs,
        check_vma=False,
    )
```

```python
import functools
import jax
import jax.numpy as jnp
from jax import lax
from jax.experimental import pallas as pl
from jax.experimental.pallas import tpu as pltpu
from jax.sharding import PartitionSpec as P

NC = 12
NP = 8
NK = NP + 1
NR = 3
SZONES = 3
RZONES = 8

DISP_STEP = 0.25
COURANT = 0.2
REACT_STEP = 0.2

BASE = 12
EXT = 8
HALO = 6
AHEAD = 3


def kernel(
    rows,
    lanes,
    conc_ref,
    sens_ref,
    vx_ref,
    vy_ref,
    ux_ref,
    uy_ref,
    sz_ref,
    rz_ref,
    p_ref,
    mol_ref,
    cap_ref,
    table_ref,
    exch_ref,
    stoich_ref,
    conc_out,
    sens_out,
    inbuf,
    outbuf,
    sta,
    stb,
    stc,
    xsend,
    xrecv,
    ysend,
    yrecv,
    fsend,
    frecv,
    yfields,
    cells,
    disp,
    adv,
    scale,
    rates,
    state,
    extra_d,
    extra_a,
    load_sem,
    store_sem,
    xs_sem,
    xr_sem,
    ys_sem,
    yr_sem,
    fs_sem,
    fr_sem,
    yfs_sem,
    yfr_sem,
):
    gx = lax.axis_index("gx")
    gy = lax.axis_index("gy")
    ngx = lax.axis_size("gx")
    has_lo = gx > 0
    has_hi = gx < ngx - 1
    wide = rows + 2 * (BASE - EXT)
    f32 = jnp.float32

    def load(k):
        return pltpu.make_async_copy(sens_ref.at[k - 1], inbuf.at[k], load_sem.at[k])

    load_first = pltpu.make_async_copy(conc_ref, inbuf.at[0], load_sem.at[0])
    load_first.start()
    for k in range(1, NK):
        load(k).start()

    barrier = pltpu.get_barrier_semaphore()
    pl.semaphore_signal(barrier, inc=1, device_id={"gy": 1 - gy})

    @pl.when(has_lo)
    def _():
        pl.semaphore_signal(barrier, inc=1, device_id={"gx": gx - 1})

    @pl.when(has_hi)
    def _():
        pl.semaphore_signal(barrier, inc=1, device_id={"gx": gx + 1})

    own = (
        vx_ref[...],
        vy_ref[...],
        ux_ref[...].astype(f32),
        uy_ref[...].astype(f32),
        sz_ref[...].astype(f32),
        rz_ref[...].astype(f32),
    )
    for f in range(6):
        fsend[0, HALO * f : HALO * (f + 1), :] = own[f][0:HALO]
        fsend[1, HALO * f : HALO * (f + 1), :] = own[f][rows - HALO : rows]
        cells[f, BASE : BASE + rows, :] = own[f]

    @pl.when(jnp.logical_not(has_lo))
    def _():
        xrecv[:, 0] = jnp.zeros_like(xrecv[:, 0])
        frecv[0] = jnp.zeros_like(frecv[0])

    @pl.when(jnp.logical_not(has_hi))
    def _():
        xrecv[:, 1] = jnp.zeros_like(xrecv[:, 1])
        frecv[1] = jnp.zeros_like(frecv[1])

    def x_copy(k, side):
        return pltpu.make_async_remote_copy(
            src_ref=xsend.at[k, side],
            dst_ref=xrecv.at[k, 1 - side],
            send_sem=xs_sem.at[k, side],
            recv_sem=xr_sem.at[k, 1 - side],
            device_id={"gx": gx - 1 if side == 0 else gx + 1},
        )

    def f_copy(side):
        return pltpu.make_async_remote_copy(
            src_ref=fsend.at[side],
            dst_ref=frecv.at[1 - side],
            send_sem=fs_sem.at[side],
            recv_sem=fr_sem.at[1 - side],
            device_id={"gx": gx - 1 if side == 0 else gx + 1},
        )

    ext = pl.ds(EXT, wide)

    def y_copy(stage, k):
        return pltpu.make_async_remote_copy(
            src_ref=ysend.at[stage, k],
            dst_ref=yrecv.at[stage, k],
            send_sem=ys_sem.at[stage, k],
            recv_sem=yr_sem.at[stage, k],
            device_id={"gy": 1 - gy},
        )

    yf_copy = pltpu.make_async_remote_copy(
        src_ref=cells.at[:, ext, :],
        dst_ref=yfields,
        send_sem=yfs_sem,
        recv_sem=yfr_sem,
        device_id={"gy": 1 - gy},
    )

    count = 1 + has_lo.astype(jnp.int32) + has_hi.astype(jnp.int32)
    pl.semaphore_wait(barrier, count)

    @pl.when(has_lo)
    def _():
        f_copy(0).start()

    @pl.when(has_hi)
    def _():
        f_copy(1).start()

    def send(k):
        for c in range(NC):
            xsend[k, 0, HALO * c : HALO * (c + 1), :] = inbuf[k, c, 0:HALO, :]
            xsend[k, 1, HALO * c : HALO * (c + 1), :] = inbuf[k, c, rows - HALO : rows, :]

        @pl.when(has_lo)
        def _():
            x_copy(k, 0).start()

        @pl.when(has_hi)
        def _():
            x_copy(k, 1).start()

    load_first.wait()
    send(0)

    def send_step(k, carry):
        load(k).wait()
        send(k)
        return carry

    lax.fori_loop(1, AHEAD, send_step, 0)

    @pl.when(has_lo)
    def _():
        f_copy(1).wait_recv()

    @pl.when(has_hi)
    def _():
        f_copy(0).wait_recv()

    for f in range(6):
        cells[f, BASE - HALO : BASE, :] = frecv[0, HALO * f : HALO * (f + 1), :]
        cells[f, BASE + rows : BASE + rows + HALO, :] = frecv[1, HALO * f : HALO * (f + 1), :]

    yf_copy.start()

    lane = lax.broadcasted_iota(jnp.int32, (wide, lanes), 1)
    row = lax.broadcasted_iota(jnp.int32, (wide, lanes), 0)
    even = (row % 2) == 0
    first = lane == 0
    last = lane == lanes - 1
    sent = jnp.where(gy == 0, lanes - 1, 0)
    no_lo = jnp.logical_and(first, gy == 0)
    no_hi = jnp.logical_and(last, gy == 1)
    from_lo = jnp.logical_and(last, gy == 1)
    from_hi = jnp.logical_and(first, gy == 0)
    margin = BASE - EXT
    lo_ok = jnp.where(has_lo, 1.0, 0.0)
    hi_ok = jnp.where(has_hi, 1.0, 0.0)
    valid = jnp.where(row < margin, lo_ok, jnp.where(row >= margin + rows, hi_ok, 1.0))
    fx = DISP_STEP * p_ref[0] * cells[0, ext, :]
    fy = DISP_STEP * p_ref[1] * cells[1, ext, :]
    sorb = jnp.zeros((wide, lanes), f32)
    for z in range(SZONES):
        sorb = jnp.where(cells[4, ext, :] == float(z), p_ref[5 + z], sorb)

    def coefficients(c, carry):
        m = DISP_STEP * mol_ref[c]
        cx = (fx + m) * valid
        cy = (fy + m) * valid
        cm = m * valid
        disp[0, c] = valid - 2.0 * cx - 2.0 * cy - cm
        disp[1, c] = cx
        disp[2, c] = cm
        disp[3, c] = jnp.where(no_lo, 0.0, cy)
        disp[4, c] = jnp.where(no_hi, 0.0, cy)
        scale[c] = valid * COURANT / (1.0 + sorb * cap_ref[c])
        for stage in range(2):
            extra_d[stage, 0, c] = jnp.zeros((wide, lanes), f32)
        return carry

    lax.fori_loop(0, NC, coefficients, 0)
    for r in range(NR):
        rate = jnp.zeros((wide, lanes), f32)
        for z in range(RZONES):
            rate = jnp.where(cells[5, ext, :] == float(z), table_ref[r, z], rate)
        rates[r] = rate

    def pack(acc, v, c):
        moved = pltpu.roll(v, c, 1) if c > 0 else v
        return jnp.where(lane == lax.rem(sent + c, lanes), moved, acc)

    def y_near(v, stage, k, c, span, cut):
        other = yrecv[stage, k, span, :]
        if c > 0:
            other = pltpu.roll(other, lanes - c, 1)
        low = pltpu.roll(jnp.where(from_lo[cut], other, v), 1, 1)
        high = pltpu.roll(jnp.where(from_hi[cut], other, v), lanes - 1, 1)
        return low, high

    def enter(k):
        @pl.when(has_lo)
        def _():
            x_copy(k, 1).wait_recv()

        @pl.when(has_hi)
        def _():
            x_copy(k, 0).wait_recv()

        acc = jnp.zeros((wide, lanes), f32)
        for c in range(NC):
            sta[k, c, BASE : BASE + rows, :] = inbuf[k, c]
            sta[k, c, BASE - HALO : BASE, :] = xrecv[k, 0, HALO * c : HALO * (c + 1), :]
            sta[k, c, BASE + rows : BASE + rows + HALO, :] = xrecv[k, 1, HALO * c : HALO * (c + 1), :]
            acc = pack(acc, sta[k, c, ext, :], c)
        ysend[0, k] = acc
        y_copy(0, k).start()

        @pl.when(k + AHEAD < NK)
        def _():
            load(k + AHEAD).wait()
            send(k + AHEAD)

    def disperse(src, stage, which, k, start, count, put):
        y_copy(stage, k).wait_recv()
        inside = pl.ds(start - EXT, count)
        cut = slice(start - EXT, start - EXT + count)

        def near(c, kk):
            v = src[kk, c, start : start + count, :]
            sx = src[kk, c, start - 2 : start - 2 + count, :] + src[kk, c, start + 2 : start + 2 + count, :]
            return v, sx

        @pl.when(k == 0)
        def _():
            for c in range(NC):
                v, sx = near(c, 0)
                yl, yh = y_near(v, stage, 0, c, inside, cut)
                lap_y = jnp.where(no_lo[cut], 0.0, yl) + jnp.where(no_hi[cut], 0.0, yh) - 2.0 * v
                part = DISP_STEP * valid[cut]
                extra_d[which, 1, c, inside, :] = part * cells[0, start : start + count, :] * (sx - 2.0 * v)
                extra_d[which, 2, c, inside, :] = part * cells[1, start : start + count, :] * lap_y

        index = jnp.where(k == 1, 1, jnp.where(k == 2, 2, 0))
        acc = jnp.zeros((count, lanes), f32)
        for c in range(NC):
            v, sx = near(c, k)
            yl, yh = y_near(v, stage, k, c, inside, cut)
            other = jnp.where(
                even[cut],
                src[k, c, start + 1 : start + 1 + count, :],
                src[k, c, start - 1 : start - 1 + count, :],
            )
            out = (
                disp[0, c, inside, :] * v
                + disp[1, c, inside, :] * sx
                + disp[2, c, inside, :] * other
                + disp[3, c, inside, :] * yl
                + disp[4, c, inside, :] * yh
                + extra_d[which, index, c, inside, :]
            )
            put(k, c, out)
            if which == 0:
                acc = pack(acc, out, c)
        if which == 0:
            ysend[1, k] = acc
            y_copy(1, k).start()

    def put_stb(k, c, out):
        stb[k, c, ext, :] = out

    def put_out(k, c, out):
        outbuf[k, c] = out

    def advection_fields():
        keep = jnp.where(gy == 0, 1.0, 0.0)
        vx, vy, ux, uy = [cells[f, ext, :] for f in range(4)]
        ahead = pl.ds(EXT + 2, wide)
        vx_next = cells[0, ahead, :]
        ux_next = cells[2, ahead, :]
        yf_copy.wait_recv()
        vy_next = jnp.where(last, keep, 1.0) * pltpu.roll(jnp.where(from_hi, yfields[1], vy), lanes - 1, 1)
        uy_next = jnp.where(last, keep, 1.0) * pltpu.roll(jnp.where(from_hi, yfields[3], uy), lanes - 1, 1)
        ayl = vy * uy
        ayh = vy_next * (1.0 - uy_next)
        adv[0] = vx_next * ux_next + vx * (1.0 - ux) + vy_next * uy_next + vy * (1.0 - uy)
        adv[1] = vx * ux
        adv[2] = vx_next * (1.0 - ux_next)
        adv[3] = jnp.where(no_lo, 0.0, ayl)
        adv[4] = jnp.where(no_hi, 0.0, ayh)

    def divergence(k, c):
        v = stb[k, c, ext, :]
        yl, yh = y_near(v, 1, k, c, slice(None), slice(None))
        div = (
            adv[0] * v
            - adv[1] * stb[k, c, EXT - 2 : EXT - 2 + wide, :]
            - adv[2] * stb[k, c, EXT + 2 : EXT + 2 + wide, :]
            - adv[3] * yl
            - adv[4] * yh
        )
        return v, div

    def advect(k):
        y_copy(1, k).wait_recv()

        @pl.when(k == 0)
        def _():
            advection_fields()
            for c in range(NC):
                v, div = divergence(0, c)
                step = scale[c]
                extra_a[c] = div * (cap_ref[c] / COURANT) * step * step
                if c < 2 * NR:
                    state[c] = v - step * div

        here = cells[4, ext, :] == (k - 6).astype(f32)
        for c in range(NC):
            v, div = divergence(k, c)
            stc[k, c, ext, :] = v - scale[c] * div + jnp.where(here, extra_a[c], 0.0)

        half = jnp.where(k == 0, 0.5, 1.0)
        for start, count in ((0, 24), (24, wide - 24)):
            part = pl.ds(EXT + start, count)
            inside = pl.ds(start, count)
            v = [stc[k, c, part, :] for c in range(NC)]
            q = []
            for r in range(NR):
                donor = state[2 * r, inside, :]
                accept = state[2 * r + 1, inside, :]
                rate = rates[r, inside, :]
                flag = jnp.where(k == 3 + r, 1.0, 0.0)
                both = accept * v[2 * r] + donor * v[2 * r + 1]
                q.append(rate * ((p_ref[2 + r] * half) * both + flag * (donor * accept)))
            for c in range(NC):
                acc = exch_ref[c, 0] * v[0]
                for d in range(1, NC):
                    acc = acc + exch_ref[c, d] * v[d]
                for r in range(NR):
                    acc = acc + stoich_ref[r, c] * q[r]
                stc[k, c, part, :] = v[c] + REACT_STEP * acc

        acc = jnp.zeros((wide, lanes), f32)
        for c in range(NC):
            acc = pack(acc, stc[k, c, ext, :], c)
        ysend[2, k] = acc
        y_copy(2, k).start()

    def store_first():
        return pltpu.make_async_copy(outbuf.at[0], conc_out, store_sem.at[0])

    def store(k):
        return pltpu.make_async_copy(outbuf.at[k], sens_out.at[k - 1], store_sem.at[k])

    def leave(k):
        disperse(stc, 2, 1, k, BASE, rows, put_out)

        @pl.when(k == 0)
        def _():
            store_first().start()

        @pl.when(k > 0)
        def _():
            store(k).start()

    def turn(t, carry):
        @pl.when(t < NK)
        def _():
            enter(t)

        @pl.when(jnp.logical_and(t >= 1, t < NK + 1))
        def _():
            disperse(sta, 0, 0, t - 1, EXT, wide, put_stb)

        @pl.when(jnp.logical_and(t >= 2, t < NK + 2))
        def _():
            advect(t - 2)

        @pl.when(t >= 3)
        def _():
            leave(t - 3)

        return carry

    lax.fori_loop(0, NK + 3, turn, 0)

    def finish(k, carry):
        for stage in range(3):
            y_copy(stage, k).wait_send()

        @pl.when(has_lo)
        def _():
            x_copy(k, 0).wait_send()

        @pl.when(has_hi)
        def _():
            x_copy(k, 1).wait_send()

        return carry

    lax.fori_loop(0, NK, finish, 0)
    yf_copy.wait_send()

    @pl.when(has_lo)
    def _():
        f_copy(0).wait_send()

    @pl.when(has_hi)
    def _():
        f_copy(1).wait_send()

    store_first().wait()
    for k in range(1, NK):
        store(k).wait()


def on_device(
    conc,
    sens,
    vel_x,
    vel_y,
    up_x,
    up_y,
    sorb_zone,
    rate_zone,
    param_values,
    mol_diff,
    sorb_cap,
    rate_table,
    exch_matrix,
    stoich,
):
    nx, layers, ny = vel_x.shape
    rows = nx * layers
    wide = rows + 2 * (BASE - EXT)
    tall = rows + 2 * BASE
    flat = lambda a: a.reshape(a.shape[:-3] + (rows, ny))
    vmem = pl.BlockSpec(memory_space=pltpu.VMEM)
    smem = pl.BlockSpec(memory_space=pltpu.SMEM)
    hbm = pl.BlockSpec(memory_space=pl.ANY)
    f32 = jnp.float32
    dma = pltpu.SemaphoreType.DMA
    conc_out, sens_out = pl.pallas_call(
        functools.partial(kernel, rows, ny),
        out_shape=(
            jax.ShapeDtypeStruct((NC, rows, ny), f32),
            jax.ShapeDtypeStruct((NP, NC, rows, ny), f32),
        ),
        in_specs=[hbm, hbm] + [vmem] * 6 + [smem] * 6,
        out_specs=(hbm, hbm),
        scratch_shapes=[
            pltpu.VMEM((NK, NC, rows, ny), f32),
            pltpu.VMEM((NK, NC, rows, ny), f32),
            pltpu.VMEM((NK, NC, tall, ny), f32),
            pltpu.VMEM((NK, NC, tall, ny), f32),
            pltpu.VMEM((NK, NC, tall, ny), f32),
            pltpu.VMEM((NK, 2, HALO * NC, ny), f32),
            pltpu.VMEM((NK, 2, HALO * NC, ny), f32),
            pltpu.VMEM((3, NK, wide, ny), f32),
            pltpu.VMEM((3, NK, wide, ny), f32),
            pltpu.VMEM((2, 40, ny), f32),
            pltpu.VMEM((2, 40, ny), f32),
            pltpu.VMEM((6, wide, ny), f32),
            pltpu.VMEM((6, tall, ny), f32),
            pltpu.VMEM((5, NC, wide, ny), f32),
            pltpu.VMEM((5, wide, ny), f32),
            pltpu.VMEM((NC, wide, ny), f32),
            pltpu.VMEM((NR, wide, ny), f32),
            pltpu.VMEM((2 * NR, wide, ny), f32),
            pltpu.VMEM((2, 3, NC, wide, ny), f32),
            pltpu.VMEM((NC, wide, ny), f32),
            dma((NK,)),
            dma((NK,)),
            dma((NK, 2)),
            dma((NK, 2)),
            dma((3, NK)),
            dma((3, NK)),
            dma((2,)),
            dma((2,)),
            dma,
            dma,
        ],
        compiler_params=pltpu.CompilerParams(
            collective_id=0, has_side_effects=True, vmem_limit_bytes=62 * 1024 * 1024
        ),
    )(
        flat(conc),
        flat(sens),
        flat(vel_x),
        flat(vel_y),
        flat(up_x),
        flat(up_y),
        flat(sorb_zone),
        flat(rate_zone),
        param_values,
        mol_diff,
        sorb_cap,
        jnp.transpose(rate_table),
        exch_matrix,
        jnp.transpose(stoich),
    )
    return conc_out.reshape(conc.shape), sens_out.reshape(sens.shape)


def solution(mesh):
    cell = P(("parts", "gx"), None, "gy")
    outs = (P(None, ("parts", "gx"), None, "gy"), P(None, None, ("parts", "gx"), None, "gy"))
    return jax.shard_map(
        on_device,
        mesh=mesh,
        in_specs=outs + (cell,) * 6 + (P(),) * 6,
        out_specs=outs,
        check_vma=False,
    )
```

```python
import functools
import jax
import jax.numpy as jnp
from jax import lax
from jax.experimental import pallas as pl
from jax.experimental.pallas import tpu as pltpu
from jax.sharding import PartitionSpec as P

NC = 12
NP = 8
NK = NP + 1
NR = 3
SZONES = 3
RZONES = 8

DISP_STEP = 0.25
COURANT = 0.2
REACT_STEP = 0.2

BASE = 12
EXT = 8
HALO = 6
AHEAD = 3


def kernel(
    rows,
    lanes,
    conc_ref,
    sens_ref,
    vx_ref,
    vy_ref,
    ux_ref,
    uy_ref,
    sz_ref,
    rz_ref,
    p_ref,
    mol_ref,
    cap_ref,
    table_ref,
    exch_ref,
    stoich_ref,
    conc_out,
    sens_out,
    inbuf,
    outbuf,
    sta,
    stb,
    stc,
    xsend,
    xrecv,
    ysend,
    ypack,
    yrecv,
    fsend,
    frecv,
    yfields,
    cells,
    disp,
    adv,
    scale,
    rates,
    state,
    extra_d,
    extra_a,
    load_sem,
    store_sem,
    xs_sem,
    xr_sem,
    ys_sem,
    yr_sem,
    fs_sem,
    fr_sem,
    yfs_sem,
    yfr_sem,
):
    gx = lax.axis_index("gx")
    gy = lax.axis_index("gy")
    ngx = lax.axis_size("gx")
    has_lo = gx > 0
    has_hi = gx < ngx - 1
    wide = rows + 2 * (BASE - EXT)
    f32 = jnp.float32

    def load(k):
        return pltpu.make_async_copy(sens_ref.at[k - 1], inbuf.at[k], load_sem.at[k])

    load_first = pltpu.make_async_copy(conc_ref, inbuf.at[0], load_sem.at[0])
    load_first.start()
    for k in range(1, NK):
        load(k).start()

    barrier = pltpu.get_barrier_semaphore()
    pl.semaphore_signal(barrier, inc=1, device_id={"gy": 1 - gy})

    @pl.when(has_lo)
    def _():
        pl.semaphore_signal(barrier, inc=1, device_id={"gx": gx - 1})

    @pl.when(has_hi)
    def _():
        pl.semaphore_signal(barrier, inc=1, device_id={"gx": gx + 1})

    own = (
        vx_ref[...],
        vy_ref[...],
        ux_ref[...].astype(f32),
        uy_ref[...].astype(f32),
        sz_ref[...].astype(f32),
        rz_ref[...].astype(f32),
    )
    for f in range(6):
        fsend[0, HALO * f : HALO * (f + 1), :] = own[f][0:HALO]
        fsend[1, HALO * f : HALO * (f + 1), :] = own[f][rows - HALO : rows]
        cells[f, BASE : BASE + rows, :] = own[f]

    @pl.when(jnp.logical_not(has_lo))
    def _():
        xrecv[:, 0] = jnp.zeros_like(xrecv[:, 0])
        frecv[0] = jnp.zeros_like(frecv[0])

    @pl.when(jnp.logical_not(has_hi))
    def _():
        xrecv[:, 1] = jnp.zeros_like(xrecv[:, 1])
        frecv[1] = jnp.zeros_like(frecv[1])

    def x_copy(k, side):
        return pltpu.make_async_remote_copy(
            src_ref=xsend.at[k, side],
            dst_ref=xrecv.at[k, 1 - side],
            send_sem=xs_sem.at[k, side],
            recv_sem=xr_sem.at[k, 1 - side],
            device_id={"gx": gx - 1 if side == 0 else gx + 1},
        )

    def f_copy(side):
        return pltpu.make_async_remote_copy(
            src_ref=fsend.at[side],
            dst_ref=frecv.at[1 - side],
            send_sem=fs_sem.at[side],
            recv_sem=fr_sem.at[1 - side],
            device_id={"gx": gx - 1 if side == 0 else gx + 1},
        )

    ext = pl.ds(EXT, wide)

    def y_copy(stage, k):
        return pltpu.make_async_remote_copy(
            src_ref=ysend.at[k] if stage == 0 else (stb, stc)[stage - 1].at[k, :, ext, :],
            dst_ref=ypack.at[k] if stage == 0 else yrecv.at[stage - 1, k],
            send_sem=ys_sem.at[stage, k],
            recv_sem=yr_sem.at[stage, k],
            device_id={"gy": 1 - gy},
        )

    yf_copy = pltpu.make_async_remote_copy(
        src_ref=cells.at[:, ext, :],
        dst_ref=yfields,
        send_sem=yfs_sem,
        recv_sem=yfr_sem,
        device_id={"gy": 1 - gy},
    )

    count = 1 + has_lo.astype(jnp.int32) + has_hi.astype(jnp.int32)
    pl.semaphore_wait(barrier, count)

    @pl.when(has_lo)
    def _():
        f_copy(0).start()

    @pl.when(has_hi)
    def _():
        f_copy(1).start()

    def send(k):
        for c in range(NC):
            xsend[k, 0, HALO * c : HALO * (c + 1), :] = inbuf[k, c, 0:HALO, :]
            xsend[k, 1, HALO * c : HALO * (c + 1), :] = inbuf[k, c, rows - HALO : rows, :]

        @pl.when(has_lo)
        def _():
            x_copy(k, 0).start()

        @pl.when(has_hi)
        def _():
            x_copy(k, 1).start()

    load_first.wait()
    send(0)

    def send_step(k, carry):
        load(k).wait()
        send(k)
        return carry

    lax.fori_loop(1, AHEAD, send_step, 0)

    @pl.when(has_lo)
    def _():
        f_copy(1).wait_recv()

    @pl.when(has_hi)
    def _():
        f_copy(0).wait_recv()

    for f in range(6):
        cells[f, BASE - HALO : BASE, :] = frecv[0, HALO * f : HALO * (f + 1), :]
        cells[f, BASE + rows : BASE + rows + HALO, :] = frecv[1, HALO * f : HALO * (f + 1), :]

    yf_copy.start()

    lane = lax.broadcasted_iota(jnp.int32, (wide, lanes), 1)
    row = lax.broadcasted_iota(jnp.int32, (wide, lanes), 0)
    even = (row % 2) == 0
    first = lane == 0
    last = lane == lanes - 1
    sent = jnp.where(gy == 0, lanes - 1, 0)
    no_lo = jnp.logical_and(first, gy == 0)
    no_hi = jnp.logical_and(last, gy == 1)
    from_lo = jnp.logical_and(last, gy == 1)
    from_hi = jnp.logical_and(first, gy == 0)
    margin = BASE - EXT
    lo_ok = jnp.where(has_lo, 1.0, 0.0)
    hi_ok = jnp.where(has_hi, 1.0, 0.0)
    valid = jnp.where(row < margin, lo_ok, jnp.where(row >= margin + rows, hi_ok, 1.0))
    fx = DISP_STEP * p_ref[0] * cells[0, ext, :]
    fy = DISP_STEP * p_ref[1] * cells[1, ext, :]
    sorb = jnp.zeros((wide, lanes), f32)
    for z in range(SZONES):
        sorb = jnp.where(cells[4, ext, :] == float(z), p_ref[5 + z], sorb)

    def coefficients(c, carry):
        m = DISP_STEP * mol_ref[c]
        cx = (fx + m) * valid
        cy = (fy + m) * valid
        cm = m * valid
        disp[0, c] = valid - 2.0 * cx - 2.0 * cy - cm
        disp[1, c] = cx
        disp[2, c] = cm
        disp[3, c] = jnp.where(no_lo, 0.0, cy)
        disp[4, c] = jnp.where(no_hi, 0.0, cy)
        scale[c] = valid * COURANT / (1.0 + sorb * cap_ref[c])
        for stage in range(2):
            extra_d[stage, 0, c] = jnp.zeros((wide, lanes), f32)
        return carry

    lax.fori_loop(0, NC, coefficients, 0)
    for r in range(NR):
        rate = jnp.zeros((wide, lanes), f32)
        for z in range(RZONES):
            rate = jnp.where(cells[5, ext, :] == float(z), table_ref[r, z], rate)
        rates[r] = rate

    def pack(acc, v, c):
        moved = pltpu.roll(v, c, 1) if c > 0 else v
        return jnp.where(lane == lax.rem(sent + c, lanes), moved, acc)

    def y_near(v, stage, k, c, span, cut):
        if stage == 0:
            other = ypack[k, span, :]
            if c > 0:
                other = pltpu.roll(other, lanes - c, 1)
        else:
            other = yrecv[stage - 1, k, c, span, :]
        low = pltpu.roll(jnp.where(from_lo[cut], other, v), 1, 1)
        high = pltpu.roll(jnp.where(from_hi[cut], other, v), lanes - 1, 1)
        return low, high

    def enter(k):
        @pl.when(has_lo)
        def _():
            x_copy(k, 1).wait_recv()

        @pl.when(has_hi)
        def _():
            x_copy(k, 0).wait_recv()

        acc = jnp.zeros((wide, lanes), f32)
        for c in range(NC):
            sta[k, c, BASE : BASE + rows, :] = inbuf[k, c]
            sta[k, c, BASE - HALO : BASE, :] = xrecv[k, 0, HALO * c : HALO * (c + 1), :]
            sta[k, c, BASE + rows : BASE + rows + HALO, :] = xrecv[k, 1, HALO * c : HALO * (c + 1), :]
            acc = pack(acc, sta[k, c, ext, :], c)
        ysend[k] = acc
        y_copy(0, k).start()

        @pl.when(k + AHEAD < NK)
        def _():
            load(k + AHEAD).wait()
            send(k + AHEAD)

    def disperse(src, stage, which, k, start, count, put):
        y_copy(stage, k).wait_recv()
        inside = pl.ds(start - EXT, count)
        cut = slice(start - EXT, start - EXT + count)

        def near(c, kk):
            v = src[kk, c, start : start + count, :]
            sx = src[kk, c, start - 2 : start - 2 + count, :] + src[kk, c, start + 2 : start + 2 + count, :]
            return v, sx

        @pl.when(k == 0)
        def _():
            for c in range(NC):
                v, sx = near(c, 0)
                yl, yh = y_near(v, stage, 0, c, inside, cut)
                lap_y = jnp.where(no_lo[cut], 0.0, yl) + jnp.where(no_hi[cut], 0.0, yh) - 2.0 * v
                part = DISP_STEP * valid[cut]
                extra_d[which, 1, c, inside, :] = part * cells[0, start : start + count, :] * (sx - 2.0 * v)
                extra_d[which, 2, c, inside, :] = part * cells[1, start : start + count, :] * lap_y

        index = jnp.where(k == 1, 1, jnp.where(k == 2, 2, 0))
        for c in range(NC):
            v, sx = near(c, k)
            yl, yh = y_near(v, stage, k, c, inside, cut)
            other = jnp.where(
                even[cut],
                src[k, c, start + 1 : start + 1 + count, :],
                src[k, c, start - 1 : start - 1 + count, :],
            )
            out = (
                disp[0, c, inside, :] * v
                + disp[1, c, inside, :] * sx
                + disp[2, c, inside, :] * other
                + disp[3, c, inside, :] * yl
                + disp[4, c, inside, :] * yh
                + extra_d[which, index, c, inside, :]
            )
            put(k, c, out)
        if which == 0:
            y_copy(1, k).start()

    def put_stb(k, c, out):
        stb[k, c, ext, :] = out

    def put_out(k, c, out):
        outbuf[k, c] = out

    def advection_fields():
        keep = jnp.where(gy == 0, 1.0, 0.0)
        vx, vy, ux, uy = [cells[f, ext, :] for f in range(4)]
        ahead = pl.ds(EXT + 2, wide)
        vx_next = cells[0, ahead, :]
        ux_next = cells[2, ahead, :]
        yf_copy.wait_recv()
        vy_next = jnp.where(last, keep, 1.0) * pltpu.roll(jnp.where(from_hi, yfields[1], vy), lanes - 1, 1)
        uy_next = jnp.where(last, keep, 1.0) * pltpu.roll(jnp.where(from_hi, yfields[3], uy), lanes - 1, 1)
        ayl = vy * uy
        ayh = vy_next * (1.0 - uy_next)
        adv[0] = vx_next * ux_next + vx * (1.0 - ux) + vy_next * uy_next + vy * (1.0 - uy)
        adv[1] = vx * ux
        adv[2] = vx_next * (1.0 - ux_next)
        adv[3] = jnp.where(no_lo, 0.0, ayl)
        adv[4] = jnp.where(no_hi, 0.0, ayh)

    def divergence(k, c):
        v = stb[k, c, ext, :]
        yl, yh = y_near(v, 1, k, c, slice(None), slice(None))
        div = (
            adv[0] * v
            - adv[1] * stb[k, c, EXT - 2 : EXT - 2 + wide, :]
            - adv[2] * stb[k, c, EXT + 2 : EXT + 2 + wide, :]
            - adv[3] * yl
            - adv[4] * yh
        )
        return v, div

    def advect(k):
        y_copy(1, k).wait_recv()

        @pl.when(k == 0)
        def _():
            advection_fields()
            for c in range(NC):
                v, div = divergence(0, c)
                step = scale[c]
                extra_a[c] = div * (cap_ref[c] / COURANT) * step * step
                if c < 2 * NR:
                    state[c] = v - step * div

        here = cells[4, ext, :] == (k - 6).astype(f32)
        for c in range(NC):
            v, div = divergence(k, c)
            stc[k, c, ext, :] = v - scale[c] * div + jnp.where(here, extra_a[c], 0.0)

        half = jnp.where(k == 0, 0.5, 1.0)
        for start, count in ((0, 24), (24, wide - 24)):
            part = pl.ds(EXT + start, count)
            inside = pl.ds(start, count)
            v = [stc[k, c, part, :] for c in range(NC)]
            q = []
            for r in range(NR):
                donor = state[2 * r, inside, :]
                accept = state[2 * r + 1, inside, :]
                rate = rates[r, inside, :]
                flag = jnp.where(k == 3 + r, 1.0, 0.0)
                both = accept * v[2 * r] + donor * v[2 * r + 1]
                q.append(rate * ((p_ref[2 + r] * half) * both + flag * (donor * accept)))
            for c in range(NC):
                acc = exch_ref[c, 0] * v[0]
                for d in range(1, NC):
                    acc = acc + exch_ref[c, d] * v[d]
                for r in range(NR):
                    acc = acc + stoich_ref[r, c] * q[r]
                stc[k, c, part, :] = v[c] + REACT_STEP * acc

        y_copy(2, k).start()

    def store_first():
        return pltpu.make_async_copy(outbuf.at[0], conc_out, store_sem.at[0])

    def store(k):
        return pltpu.make_async_copy(outbuf.at[k], sens_out.at[k - 1], store_sem.at[k])

    def leave(k):
        disperse(stc, 2, 1, k, BASE, rows, put_out)

        @pl.when(k == 0)
        def _():
            store_first().start()

        @pl.when(k > 0)
        def _():
            store(k).start()

    def turn(t, carry):
        @pl.when(t < NK)
        def _():
            enter(t)

        @pl.when(jnp.logical_and(t >= 1, t < NK + 1))
        def _():
            disperse(sta, 0, 0, t - 1, EXT, wide, put_stb)

        @pl.when(jnp.logical_and(t >= 2, t < NK + 2))
        def _():
            advect(t - 2)

        @pl.when(t >= 3)
        def _():
            leave(t - 3)

        return carry

    lax.fori_loop(0, NK + 3, turn, 0)

    def finish(k, carry):
        for stage in range(3):
            y_copy(stage, k).wait_send()

        @pl.when(has_lo)
        def _():
            x_copy(k, 0).wait_send()

        @pl.when(has_hi)
        def _():
            x_copy(k, 1).wait_send()

        return carry

    lax.fori_loop(0, NK, finish, 0)
    yf_copy.wait_send()

    @pl.when(has_lo)
    def _():
        f_copy(0).wait_send()

    @pl.when(has_hi)
    def _():
        f_copy(1).wait_send()

    store_first().wait()
    for k in range(1, NK):
        store(k).wait()


def on_device(
    conc,
    sens,
    vel_x,
    vel_y,
    up_x,
    up_y,
    sorb_zone,
    rate_zone,
    param_values,
    mol_diff,
    sorb_cap,
    rate_table,
    exch_matrix,
    stoich,
):
    nx, layers, ny = vel_x.shape
    rows = nx * layers
    wide = rows + 2 * (BASE - EXT)
    tall = rows + 2 * BASE
    flat = lambda a: a.reshape(a.shape[:-3] + (rows, ny))
    vmem = pl.BlockSpec(memory_space=pltpu.VMEM)
    smem = pl.BlockSpec(memory_space=pltpu.SMEM)
    hbm = pl.BlockSpec(memory_space=pl.ANY)
    f32 = jnp.float32
    dma = pltpu.SemaphoreType.DMA
    conc_out, sens_out = pl.pallas_call(
        functools.partial(kernel, rows, ny),
        out_shape=(
            jax.ShapeDtypeStruct((NC, rows, ny), f32),
            jax.ShapeDtypeStruct((NP, NC, rows, ny), f32),
        ),
        in_specs=[hbm, hbm] + [vmem] * 6 + [smem] * 6,
        out_specs=(hbm, hbm),
        scratch_shapes=[
            pltpu.VMEM((NK, NC, rows, ny), f32),
            pltpu.VMEM((NK, NC, rows, ny), f32),
            pltpu.VMEM((NK, NC, tall, ny), f32),
            pltpu.VMEM((NK, NC, tall, ny), f32),
            pltpu.VMEM((NK, NC, tall, ny), f32),
            pltpu.VMEM((NK, 2, HALO * NC, ny), f32),
            pltpu.VMEM((NK, 2, HALO * NC, ny), f32),
            pltpu.VMEM((NK, wide, ny), f32),
            pltpu.VMEM((NK, wide, ny), f32),
            pltpu.VMEM((2, NK, NC, wide, ny), f32),
            pltpu.VMEM((2, 40, ny), f32),
            pltpu.VMEM((2, 40, ny), f32),
            pltpu.VMEM((6, wide, ny), f32),
            pltpu.VMEM((6, tall, ny), f32),
            pltpu.VMEM((5, NC, wide, ny), f32),
            pltpu.VMEM((5, wide, ny), f32),
            pltpu.VMEM((NC, wide, ny), f32),
            pltpu.VMEM((NR, wide, ny), f32),
            pltpu.VMEM((2 * NR, wide, ny), f32),
            pltpu.VMEM((2, 3, NC, wide, ny), f32),
            pltpu.VMEM((NC, wide, ny), f32),
            dma((NK,)),
            dma((NK,)),
            dma((NK, 2)),
            dma((NK, 2)),
            dma((3, NK)),
            dma((3, NK)),
            dma((2,)),
            dma((2,)),
            dma,
            dma,
        ],
        compiler_params=pltpu.CompilerParams(
            collective_id=0, has_side_effects=True, vmem_limit_bytes=62 * 1024 * 1024
        ),
    )(
        flat(conc),
        flat(sens),
        flat(vel_x),
        flat(vel_y),
        flat(up_x),
        flat(up_y),
        flat(sorb_zone),
        flat(rate_zone),
        param_values,
        mol_diff,
        sorb_cap,
        jnp.transpose(rate_table),
        exch_matrix,
        jnp.transpose(stoich),
    )
    return conc_out.reshape(conc.shape), sens_out.reshape(sens.shape)


def solution(mesh):
    cell = P(("parts", "gx"), None, "gy")
    outs = (P(None, ("parts", "gx"), None, "gy"), P(None, None, ("parts", "gx"), None, "gy"))
    return jax.shard_map(
        on_device,
        mesh=mesh,
        in_specs=outs + (cell,) * 6 + (P(),) * 6,
        out_specs=outs,
        check_vma=False,
    )
```
